32 devices in a mesh: grp: 2 (over x), seq: 8 (over z, y), head: 2 (over core).
Axes of the slice: x: 2, y: 2, z: 4, core: 2. Of those that a mesh axis runs over, the one named last changes fastest.
Arguments:
- q_nope: bfloat16 [8, 128, 128], P('grp', ('seq', 'head')), parts along dimension 0, may hold values from -6 to 6
- q_rope: bfloat16 [8, 128, 64], P('grp', ('seq', 'head')), parts along dimension 0, may hold values from -150 to 150
- w_uk: bfloat16 [128, 128, 512], P(('seq', 'head')), may hold values from -0.5 to 0.5
- w_uv: bfloat16 [128, 512, 128], P(('seq', 'head')), may hold values from -1 to 1
- cache: bfloat16 [8, 4096, 576], P('grp', 'seq'), parts along dimension 0, may hold values from -12 to 12
- lengths: int32 [8], P('grp'), parts along dimension 0, may hold values from 2048 to 4096, as said below
- selected: int32 [8, 8, 32], P('grp'), parts along dimension 0, may hold values from 0 to 63, as said below
Outputs:
- attended: bfloat16 [8, 128, 128], P('grp', ('seq', 'head')), parts along dimension 0
- bounds: float32 [8, 8, 64], P('grp', None, 'seq'), parts along dimension 0
The draws below stay inside these ranges and needn't reach their ends.
There are 2 independent parts, one for each index of `grp`. The reference program is written for one: setup_inputs(seed, part) draws one part's arguments, and reference() takes and returns one part's arrays. A program takes and returns all parts, laid end to end along the dimension named above; an argument that names none is the same for every part. Nothing has to cross between parts.
Inputs may be any that keep to these rules, and one draw needn't show every extreme that they name: `lengths`: some request has exactly 4096 cached tokens; every request has 2048 or more. `selected`: for each request and head group the 32 page numbers are distinct and below ceil(lengths[r] / 64); page 0 and the page of the request's last cached token are always among them.
All inputs are finite; a program needn't handle non-finite values.
Results may differ from the reference program's by a relative error of at most 0.0065.
Values may be sent and summed in bfloat16 or wider, within the bound.
No kernel may reach another device: no remote copies, remote signals or barrier semaphores. Data moves between devices by JAX's collectives and lax.ppermute only.
A program may use at most 64 MiB of HBM per device.

```python
import jax
import jax.numpy as jnp
from jax import lax

H = 128
DN = 128
DR = 64
DL = 512
DV = 128
GH = 16
PAGE = 64
SEL = 32
R = 4
NG = 8
PAGES = 64
L = 4096


def shared_lengths(key):
    uniform_len = jax.random.randint(jax.random.fold_in(key, 11), (R,), SEL * PAGE, L + 1)
    longest = jax.random.randint(jax.random.fold_in(key, 12), (), 0, R)
    return jnp.where(jnp.arange(R) == longest, L, uniform_len).astype(jnp.int32)


def draw_lengths(key, part):
    return shared_lengths(key)


def draw_selected(key, part):
    request_len = shared_lengths(key)
    pages_used = (request_len + PAGE - 1) // PAGE
    subkeys = jax.random.split(jax.random.fold_in(key, 13), R * NG)

    def shuffle(subkey):
        return jax.random.permutation(subkey, PAGES)
    shuffled = jax.vmap(shuffle)(subkeys).reshape(R, NG, PAGES).astype(jnp.int32)
    page_number = jnp.arange(PAGES, dtype=jnp.int32)[None, None, :]
    ranking = jnp.where(page_number >= pages_used[:, None, None], shuffled + 2 * PAGES, shuffled)
    ranking = jnp.where(page_number == 0, -2, ranking)
    ranking = jnp.where(page_number == (pages_used - 1)[:, None, None], -1, ranking)
    ordering = jnp.argsort(ranking, axis=-1, stable=True)
    return ordering[:, :, :SEL].astype(jnp.int32)


def draw_cache(key, part):
    anchor = jax.random.fold_in(key, 31)
    latent = jnp.clip(jax.random.normal(jax.random.fold_in(anchor, 2), (R, L, DL), jnp.float32), -6.0, 6.0)
    rotary = jnp.clip(jax.random.normal(jax.random.fold_in(anchor, 3), (R, L, DR), jnp.float32), -6.0, 6.0)
    return jnp.concatenate([latent, rotary], axis=2).astype(jnp.bfloat16)


def draw_q_rope(key, part):
    anchor = jax.random.fold_in(key, 41)
    jitter = jax.random.normal(jax.random.fold_in(anchor, 1), (R, H, DR), jnp.float32)
    values = jnp.clip(jitter, -6.0, 6.0)
    return values.astype(jnp.bfloat16)


def levels(own_key, dims, pieces, low, high):
    def one(position, blocks):
        heights = jax.random.uniform(jax.random.fold_in(jax.random.fold_in(own_key, 6), position), (blocks,), jnp.float32, low / len(pieces), high / len(pieces))
        return jnp.repeat(jnp.exp(heights), dims[position] // blocks).reshape((-1,) + (1,) * (len(dims) - position - 1))

    factor_of = one(*pieces[0])
    for cut in pieces[1:]:
        factor_of = factor_of * one(*cut)
    return factor_of


def scatter_about(rng, shape, scale, most, shards=(), held_as=jnp.bfloat16):
    factor_of = levels(rng, shape, shards, -0.22, 0.18) if shards else 1.0
    values = jax.random.normal(rng, shape, jnp.float32) * scale * factor_of
    return jnp.minimum(jnp.maximum(values, -most), most).astype(held_as)


def setup_inputs(seed: int = 0, part: int = 0) -> dict:
    streams_of = jax.random.split(jax.random.key(seed), 8)
    part_splits = jax.random.split(jax.random.fold_in(streams_of[7], part), 8)
    return {
        "q_nope": scatter_about(part_splits[0], (R, H, DN), 1.0, 6.0, ((1, 16),)),
        "q_rope": draw_q_rope(jax.random.fold_in(jax.random.fold_in(streams_of[7], part), 71), part),
        "w_uk": scatter_about(streams_of[2], (H, DN, DL), DN ** -0.5, 0.5, ((0, 16),)),
        "w_uv": scatter_about(streams_of[3], (H, DL, DV), (DL // 16) ** -0.5, 1.0, ((0, 16),)),
        "cache": draw_cache(jax.random.fold_in(jax.random.fold_in(streams_of[7], part), 71), part),
        "lengths": draw_lengths(jax.random.fold_in(jax.random.fold_in(streams_of[7], part), 71), part),
        "selected": draw_selected(jax.random.fold_in(jax.random.fold_in(streams_of[7], part), 71), part),
    }


def reference(q_nope, q_rope, w_uk, w_uv, cache, lengths, selected):
    softmax_scale = (DN + DR) ** -0.5
    query_latent = jnp.einsum("rhn,hnl->rhl", q_nope.astype(jnp.float32), w_uk.astype(jnp.float32)).astype(jnp.bfloat16)
    absorbed = jnp.concatenate([query_latent, q_rope], axis=2)

    def per_request(inputs):
        query_rows, cache_rows, length, picks = inputs
        token_index = jnp.arange(PAGES * PAGE, dtype=jnp.int32).reshape(PAGES, PAGE)
        live_token = token_index < length
        live_page = live_token[:, 0]
        page_blocks = cache_rows.reshape(PAGES, PAGE, DL + DR).astype(jnp.float32)
        page_low = jnp.min(jnp.where(live_token[..., None], page_blocks, jnp.inf), axis=1)
        page_high = jnp.max(jnp.where(live_token[..., None], page_blocks, -jnp.inf), axis=1)
        page_low = jnp.where(live_page[:, None], page_low, 0.0)
        page_high = jnp.where(live_page[:, None], page_high, 0.0)
        middle = (page_low + page_high) * 0.5
        spread = (page_high - page_low) * 0.5
        query_float = query_rows.astype(jnp.float32)
        head_bound = softmax_scale * (
            jnp.dot(query_float, middle.T, precision=lax.Precision.HIGHEST)
            + jnp.dot(jnp.abs(query_float), spread.T, precision=lax.Precision.HIGHEST))
        group_bound = jnp.max(head_bound.reshape(NG, GH, PAGES), axis=1)
        group_bound = jnp.where(live_page[None, :], group_bound, 0.0)
        chosen = page_blocks[picks]
        chosen_live = live_token[picks]
        grouped = query_float.reshape(NG, GH, DL + DR)
        scores = jnp.einsum("gkd,gspd->gksp", grouped, chosen) * softmax_scale
        scores = jnp.where(chosen_live[:, None], scores, -1e30)
        page_top = jnp.max(scores, axis=3)
        weights = jnp.where(chosen_live[:, None], jnp.exp(scores - page_top[..., None]), 0.0).astype(jnp.bfloat16)
        weights = lax.optimization_barrier(weights).astype(jnp.float32)
        page_total = jnp.sum(weights, axis=3)
        page_weighted = jnp.einsum("gksp,gspl->gksl", weights, chosen[..., :DL])
        top = jnp.max(page_top, axis=2)
        factor = jnp.exp(page_top - top[..., None])
        total = jnp.sum(factor * page_total, axis=2)
        weighted = jnp.sum(factor[..., None] * page_weighted, axis=2)
        latent_out = (weighted / total[..., None]).astype(jnp.bfloat16).reshape(H, DL)
        return latent_out, group_bound

    latent_out, bounds = lax.map(per_request, (absorbed, cache, lengths, selected))
    attended = jnp.einsum("rhl,hlv->rhv", latent_out.astype(jnp.float32), w_uv.astype(jnp.float32)).astype(jnp.bfloat16)
    return (attended, bounds)
```

```python
import functools

import jax
import jax.numpy as jnp
from jax import lax
from jax.experimental import pallas as pl
from jax.experimental.pallas import tpu as pltpu
from jax.sharding import PartitionSpec as P

GH = 16
PAGE = 64
NEG = -1e30
BF16 = jnp.bfloat16
F32 = jnp.float32
LANES = 128
VMEM = pl.BlockSpec(memory_space=pltpu.VMEM)
SMEM = pl.BlockSpec(memory_space=pltpu.SMEM)


def params(mib=24):
    return pltpu.CompilerParams(vmem_limit_bytes=mib << 20)


def absorb_kernel(nope_ref, rope_ref, w_ref, out_ref):
    requests, heads, size = nope_ref.shape
    latent = w_ref.shape[2]
    rows = requests * heads
    nope = nope_ref[...].astype(F32).reshape(rows, size)
    head = lax.broadcasted_iota(jnp.int32, (rows, size), 0) % heads
    wide = jnp.concatenate(
        [jnp.where(head == j, nope, 0.0) for j in range(heads)], axis=1
    ).astype(BF16)
    weight = w_ref[...].reshape(heads * size, latent)
    out_ref[:, :latent] = jnp.dot(wide, weight, preferred_element_type=F32).astype(BF16)
    out_ref[:, latent:] = rope_ref[...].astype(F32).reshape(rows, rope_ref.shape[2]).astype(BF16)


def split3(x):
    high = x.astype(BF16)
    rest = x - high.astype(F32)
    middle = rest.astype(BF16)
    return high, middle, (rest - middle.astype(F32)).astype(BF16)


def queries_of(blocks, request, heads):
    rows = slice(request * heads, (request + 1) * heads)
    return jnp.concatenate([b[rows] for b in blocks], axis=0)


def group_of(offset, heads):
    source = jnp.bitwise_xor(lax.axis_index("seq"), offset)
    return (source * lax.axis_size("head") + lax.axis_index("head")) * heads // GH


def attend_kernel(scale, heads, offsets, latent, *refs):
    count = len(offsets)
    block_refs = refs[:count]
    cache_ref, selected_ref, lengths_ref, send_ref, keep_ref, sum_ref, mask_ref = refs[count:]
    requests, groups, picks = selected_ref.shape
    tokens = cache_ref.shape[2]
    pages = tokens // PAGE
    rank = lax.axis_index("seq")
    blocks = [b[...].astype(F32) for b in block_refs]
    place = selected_ref[...].reshape(requests * groups, picks) - rank * pages
    here = (place >= 0) & (place < pages)
    bits = jnp.sum(
        jnp.where(here, jnp.left_shift(1, jnp.where(here, place, 0)), 0).astype(F32),
        axis=1,
        keepdims=True,
    ).astype(jnp.int32)
    lane = lax.broadcasted_iota(jnp.int32, (groups, tokens), 1)
    for r in range(requests):
        word = bits[r * groups : (r + 1) * groups]
        picked = jnp.bitwise_and(jnp.right_shift(word, lane // PAGE), 1) == 1
        live = lane + rank * tokens < lengths_ref[r]
        mask_ref[r * groups : (r + 1) * groups, :] = jnp.where(picked & live, 1.0, 0.0)
    outs, sums = [], []
    for r in range(requests):
        query = queries_of(blocks, r, heads).astype(BF16)
        keys = cache_ref[r]
        scores = jnp.dot(query, keys, preferred_element_type=F32) * scale
        mask = jnp.concatenate(
            [
                jnp.broadcast_to(
                    mask_ref[pl.ds(r * groups + group_of(k, heads), 1), :], (heads, tokens)
                )
                for k in offsets
            ],
            axis=0,
        )
        scores = jnp.where(mask > 0.5, scores, NEG)
        top = jnp.max(scores, axis=1, keepdims=True)
        weights = jnp.where(mask > 0.5, jnp.exp(scores - top), 0.0).astype(BF16)
        total = jnp.sum(weights.astype(F32), axis=1, keepdims=True)
        weighted = lax.dot_general(
            weights, keys[:latent], (((1,), (1,)), ((), ())), preferred_element_type=F32
        )
        some = total > 0.0
        safe = jnp.where(some, total, 1.0)
        outs.append(weighted / safe)
        sums.append(jnp.where(some, top + jnp.log(safe), NEG))
    for i, k in enumerate(offsets):
        rows = slice(i * heads, (i + 1) * heads)
        out = jnp.concatenate([o[rows] for o in outs], axis=0)
        lse = jnp.concatenate([s[rows] for s in sums], axis=0)
        lse = jnp.broadcast_to(lse, (lse.shape[0], LANES))
        if k % 2:
            send_ref[k // 2, :, :latent] = out.astype(BF16)
            send_ref[k // 2, :, latent:] = packed(lse)
        else:
            keep_ref[k // 2] = out
            sum_ref[k // 2] = lse


def packed(lse):
    lane = lax.broadcasted_iota(jnp.int32, lse.shape, 1)
    high, middle, low = (p.astype(F32) for p in split3(lse))
    return jnp.where(lane == 0, high, jnp.where(lane == 1, middle, low)).astype(BF16)


def unpacked(tail):
    tail = tail.astype(F32)
    return tail[:, 0:1] + tail[:, 1:2] + tail[:, 2:3]


def merge(parts):
    top = functools.reduce(jnp.maximum, [s for _, s in parts])
    factors = [jnp.exp(s - top) for _, s in parts]
    total = functools.reduce(jnp.add, factors)
    mixed = functools.reduce(jnp.add, [f * o for f, (o, _) in zip(factors, parts)])
    return mixed / total, top + jnp.log(total)


def pair_kernel(latent, got_ref, keep_ref, sum_ref, own_ref, own_sum_ref, *send_refs):
    for i in range(got_ref.shape[0]):
        got = got_ref[i]
        out, lse = merge(
            [
                (got[:, :latent].astype(F32), unpacked(got[:, latent:])),
                (keep_ref[i], sum_ref[i][:, 0:1]),
            ]
        )
        lse = jnp.broadcast_to(lse, (lse.shape[0], LANES))
        if i == 0:
            own_ref[...] = out
            own_sum_ref[...] = lse
        else:
            send_refs[i - 1][:, :latent] = out.astype(BF16)
            send_refs[i - 1][:, latent:] = packed(lse)


def value_kernel(latent, heads, own_ref, own_sum_ref, w_ref, mine_ref, other_ref, lengths_ref, *refs):
    got_refs, (out_ref, bounds_ref) = refs[:-2], refs[-2:]
    requests = out_ref.shape[0]
    parts = [(own_ref[...], own_sum_ref[...][:, 0:1])]
    for got_ref in got_refs:
        got = got_ref[...]
        parts.append((got[:, :latent].astype(F32), unpacked(got[:, latent:])))
    mixed, _ = merge(parts)
    mixed = mixed.astype(BF16).astype(F32)
    rows = mixed.shape[0]
    head = lax.broadcasted_iota(jnp.int32, (rows, latent), 0) % heads
    out = jnp.zeros((rows, w_ref.shape[2]), F32)
    for j in range(heads):
        out += jnp.dot(
            jnp.where(head == j, mixed, 0.0).astype(BF16), w_ref[j], preferred_element_type=F32
        )
    out_ref[...] = out.reshape(out_ref.shape).astype(BF16)
    groups, pages = bounds_ref.shape[1:]
    first = (
        lax.axis_index("seq") * pages + lax.broadcasted_iota(jnp.int32, (groups, pages), 1)
    ) * PAGE
    for r in range(requests):
        bounds_ref[r] = jnp.where(
            first < lengths_ref[r], jnp.maximum(mine_ref[r], other_ref[r]), 0.0
        )


def bounds_kernel(scale, heads, offsets, *refs):
    count = len(offsets)
    block_refs = refs[:count]
    cache_ref, lengths_ref, out_ref = refs[count:]
    requests, groups, pages = out_ref.shape
    width, tokens = cache_ref.shape[1:]
    rank = lax.axis_index("seq")
    blocks = [b[...].astype(F32) for b in block_refs]
    row = lax.broadcasted_iota(jnp.int32, (tokens, width), 0)
    group = lax.broadcasted_iota(jnp.int32, (groups, pages), 0)
    for r in range(requests):
        slots = cache_ref[r].astype(F32).T
        slots = slots.reshape(pages, PAGE, width)
        live = (row + rank * tokens < lengths_ref[r]).reshape(pages, PAGE, width)
        slots = jnp.where(live, slots, slots[:, 0:1, :])
        low = jnp.min(slots, axis=1).astype(BF16)
        high = jnp.max(slots, axis=1).astype(BF16)
        query = queries_of(blocks, r, heads)
        dims = (((1,), (1,)), ((), ()))
        bound = lax.dot_general(
            jnp.maximum(query, 0.0).astype(BF16), high, dims, preferred_element_type=F32
        ) + lax.dot_general(
            jnp.minimum(query, 0.0).astype(BF16), low, dims, preferred_element_type=F32
        )
        bound = bound * scale
        best = jnp.full((groups, pages), NEG, F32)
        for i, k in enumerate(offsets):
            peak = jnp.max(bound[i * heads : (i + 1) * heads], axis=0, keepdims=True)
            best = jnp.where(group == group_of(k, heads), jnp.maximum(best, peak), best)
        out_ref[r] = best


def local(q_nope, q_rope, w_uk, w_uv, cache, lengths, selected):
    seq_count = lax.axis_size("seq")
    head_count = lax.axis_size("head")
    requests, heads, _ = q_nope.shape
    latent = w_uk.shape[2]
    width = cache.shape[2]
    tokens = cache.shape[1]
    pages = tokens // PAGE
    groups = selected.shape[1]
    rows = requests * heads
    scale = (q_nope.shape[2] + q_rope.shape[2]) ** (-0.5)
    assert seq_count & (seq_count - 1) == 0 and GH % heads == 0
    offsets = tuple(range(seq_count))
    far = tuple(reversed(range(2, seq_count, 2)))
    half = seq_count // 2
    slots = jnp.swapaxes(cache, 1, 2)

    def swap(x, k):
        return lax.ppermute(x, "seq", [(i, i ^ k) for i in range(seq_count)])

    mine = pl.pallas_call(
        absorb_kernel,
        out_shape=jax.ShapeDtypeStruct((rows, width), BF16),
        in_specs=[VMEM] * 3,
        out_specs=VMEM,
        compiler_params=params(),
        name="absorb",
    )(q_nope, q_rope, w_uk)
    block = {0: mine}
    for k in far:
        block[k] = swap(mine, k)
    block[1] = swap(mine, 1)
    for k in far:
        block[k + 1] = swap(block[k], 1)
    blocks = [block[k] for k in offsets]

    send, keep, sums = pl.pallas_call(
        functools.partial(attend_kernel, scale, heads, offsets, latent),
        out_shape=(
            jax.ShapeDtypeStruct((half, rows, latent + LANES), BF16),
            jax.ShapeDtypeStruct((half, rows, latent), F32),
            jax.ShapeDtypeStruct((half, rows, LANES), F32),
        ),
        in_specs=[VMEM] * (seq_count + 2) + [SMEM],
        out_specs=(VMEM,) * 3,
        scratch_shapes=[pltpu.VMEM((requests * groups, tokens), F32)],
        compiler_params=params(),
        name="attend",
    )(*blocks, slots, selected, lengths)
    got = swap(send, 1)

    bounds = pl.pallas_call(
        functools.partial(bounds_kernel, scale, heads, offsets),
        out_shape=jax.ShapeDtypeStruct((requests, groups, pages), F32),
        in_specs=[VMEM] * (seq_count + 1) + [SMEM],
        out_specs=VMEM,
        compiler_params=params(),
        name="page_bounds",
    )(*blocks, slots, lengths)
    others = lax.ppermute(
        bounds, "head", [(i, (i + 1) % head_count) for i in range(head_count)]
    )

    shape = jax.ShapeDtypeStruct((rows, latent + LANES), BF16)
    own, own_sum, *sends = pl.pallas_call(
        functools.partial(pair_kernel, latent),
        out_shape=(
            jax.ShapeDtypeStruct((rows, latent), F32),
            jax.ShapeDtypeStruct((rows, LANES), F32),
        )
        + (shape,) * (half - 1),
        in_specs=[VMEM] * 3,
        out_specs=(VMEM,) * (half + 1),
        compiler_params=params(),
        name="merge_pair",
    )(got, keep, sums)
    gots = {k: swap(sends[k // 2 - 1], k) for k in far}

    return pl.pallas_call(
        functools.partial(value_kernel, latent, heads),
        out_shape=(
            jax.ShapeDtypeStruct((requests, heads, w_uv.shape[2]), BF16),
            jax.ShapeDtypeStruct((requests, groups, pages), F32),
        ),
        in_specs=[VMEM] * 5 + [SMEM] + [VMEM] * (half - 1),
        out_specs=(VMEM, VMEM),
        compiler_params=params(),
        name="merge_and_value",
    )(own, own_sum, w_uv, bounds, others, lengths, *[gots[k] for k in far])


def solution(mesh):
    assert mesh.shape["head"] == 2
    placed = (
        P("grp", ("seq", "head"), None),
        P("grp", ("seq", "head"), None),
        P(("seq", "head"), None, None),
        P(("seq", "head"), None, None),
        P("grp", "seq", None),
        P("grp"),
        P("grp", None, None),
    )
    return jax.shard_map(
        local,
        mesh=mesh,
        in_specs=placed,
        out_specs=(P("grp", ("seq", "head"), None), P("grp", None, "seq")),
        check_vma=False,
    )
```

```python
import functools

import jax
import jax.numpy as jnp
from jax import lax
from jax.experimental import pallas as pl
from jax.experimental.pallas import tpu as pltpu
from jax.sharding import PartitionSpec as P

GH = 16
PAGE = 64
NEG = -1e30
BF16 = jnp.bfloat16
F32 = jnp.float32
LANES = 128
VMEM = pl.BlockSpec(memory_space=pltpu.VMEM)
SMEM = pl.BlockSpec(memory_space=pltpu.SMEM)
HBM = pl.BlockSpec(memory_space=pltpu.HBM)
ANY = pl.BlockSpec(memory_space=pl.ANY)


def params(mib=24):
    return pltpu.CompilerParams(vmem_limit_bytes=mib << 20)


def absorb_kernel(nope_hbm, rope_hbm, w_hbm, out_ref, nope_ref, rope_ref, w_ref, sems):
    requests, heads, size = nope_ref.shape
    latent = w_ref.shape[2]
    rows = requests * heads
    step = 2 if heads % 2 == 0 else 1
    pieces = heads // step
    small = [
        pltpu.make_async_copy(nope_hbm, nope_ref, sems.at[pieces]),
        pltpu.make_async_copy(rope_hbm, rope_ref, sems.at[pieces + 1]),
    ]
    large = [
        pltpu.make_async_copy(
            w_hbm.at[pl.ds(i * step, step)], w_ref.at[pl.ds(i * step, step)], sems.at[i]
        )
        for i in range(pieces)
    ]
    for copy in small + large:
        copy.start()
    for copy in small:
        copy.wait()
    nope = nope_ref[...].astype(F32).reshape(rows, size)
    head = lax.broadcasted_iota(jnp.int32, (rows, size), 0) % heads
    out_ref[:, latent:] = rope_ref[...].astype(F32).reshape(rows, rope_ref.shape[2]).astype(BF16)
    total = jnp.zeros((rows, latent), F32)
    for i, copy in enumerate(large):
        wide = jnp.concatenate(
            [jnp.where(head == i * step + j, nope, 0.0) for j in range(step)], axis=1
        ).astype(BF16)
        copy.wait()
        weight = w_ref[i * step : (i + 1) * step].reshape(step * size, latent)
        total += jnp.dot(wide, weight, preferred_element_type=F32)
    out_ref[:, :latent] = total.astype(BF16)


def stage_kernel(
    cache_hbm, w_hbm, selected_hbm, lengths_hbm, after_ref,
    cache_ref, w_ref, mask_ref, low_ref, high_ref, selected_ref, lengths_ref, sems,
):
    requests, groups, picks = selected_ref.shape
    width, tokens = cache_ref.shape[1:]
    pages = tokens // PAGE
    rank = lax.axis_index("seq")
    copies = [
        pltpu.make_async_copy(selected_hbm, selected_ref, sems.at[0]),
        pltpu.make_async_copy(lengths_hbm, lengths_ref, sems.at[1]),
        *(
            pltpu.make_async_copy(cache_hbm.at[r], cache_ref.at[r], sems.at[3 + r])
            for r in range(requests)
        ),
        pltpu.make_async_copy(w_hbm, w_ref, sems.at[2]),
    ]
    for copy in copies:
        copy.start()
    copies[0].wait()
    copies[1].wait()
    place = selected_ref[...].reshape(requests * groups, picks) - rank * pages
    here = (place >= 0) & (place < pages)
    bits = jnp.sum(
        jnp.where(here, jnp.left_shift(1, jnp.where(here, place, 0)), 0).astype(F32),
        axis=1,
        keepdims=True,
    ).astype(jnp.int32)
    lane = lax.broadcasted_iota(jnp.int32, (groups, tokens), 1)
    for r in range(requests):
        word = bits[r * groups : (r + 1) * groups]
        picked = jnp.bitwise_and(jnp.right_shift(word, lane // PAGE), 1) == 1
        live = lane + rank * tokens < lengths_ref[r]
        mask_ref[r * groups : (r + 1) * groups, :] = jnp.where(picked & live, 1.0, 0.0)
    row = lax.broadcasted_iota(jnp.int32, (tokens, width), 0) + rank * tokens
    for r in range(requests):
        copies[2 + r].wait()
        slots = cache_ref[r].astype(F32).T
        live = row < lengths_ref[r]
        slots = slots.reshape(pages, PAGE, width)
        slots = jnp.where(live.reshape(pages, PAGE, width), slots, slots[:, 0:1, :])
        low_ref[r] = jnp.min(slots, axis=1)
        high_ref[r] = jnp.max(slots, axis=1)
    copies[-1].wait()


def split3(x):
    high = x.astype(BF16)
    rest = x - high.astype(F32)
    middle = rest.astype(BF16)
    return high, middle, (rest - middle.astype(F32)).astype(BF16)


def queries_of(blocks, request, heads):
    rows = slice(request * heads, (request + 1) * heads)
    return jnp.concatenate([b[rows] for b in blocks], axis=0)


def group_of(offset, heads):
    source = jnp.bitwise_xor(lax.axis_index("seq"), offset)
    return (source * lax.axis_size("head") + lax.axis_index("head")) * heads // GH


def attend_kernel(scale, heads, offsets, latent, *refs):
    count = len(offsets)
    block_refs = refs[:count]
    cache_ref, mask_ref, send_ref, keep_ref, sum_ref = refs[count:]
    requests, _, tokens = cache_ref.shape
    groups = mask_ref.shape[0] // requests
    blocks = [b[...].astype(F32) for b in block_refs]
    outs, sums = [], []
    for r in range(requests):
        query = queries_of(blocks, r, heads).astype(BF16)
        keys = cache_ref[r]
        scores = jnp.dot(query, keys, preferred_element_type=F32) * scale
        mask = jnp.concatenate(
            [
                jnp.broadcast_to(
                    mask_ref[pl.ds(r * groups + group_of(k, heads), 1), :], (heads, tokens)
                )
                for k in offsets
            ],
            axis=0,
        )
        scores = jnp.where(mask > 0.5, scores, NEG)
        top = jnp.max(scores, axis=1, keepdims=True)
        weights = jnp.where(mask > 0.5, jnp.exp(scores - top), 0.0).astype(BF16)
        total = jnp.sum(weights.astype(F32), axis=1, keepdims=True)
        weighted = lax.dot_general(
            weights, keys[:latent], (((1,), (1,)), ((), ())), preferred_element_type=F32
        )
        some = total > 0.0
        safe = jnp.where(some, total, 1.0)
        outs.append(weighted / safe)
        sums.append(jnp.where(some, top + jnp.log(safe), NEG))
    for i, k in enumerate(offsets):
        rows = slice(i * heads, (i + 1) * heads)
        out = jnp.concatenate([o[rows] for o in outs], axis=0)
        lse = jnp.concatenate([s[rows] for s in sums], axis=0)
        lse = jnp.broadcast_to(lse, (lse.shape[0], LANES))
        if k % 2:
            send_ref[k // 2, :, :latent] = out.astype(BF16)
            send_ref[k // 2, :, latent:] = packed(lse)
        else:
            keep_ref[k // 2] = out
            sum_ref[k // 2] = lse


def packed(lse):
    lane = lax.broadcasted_iota(jnp.int32, lse.shape, 1)
    high, middle, low = (p.astype(F32) for p in split3(lse))
    return jnp.where(lane == 0, high, jnp.where(lane == 1, middle, low)).astype(BF16)


def unpacked(tail):
    tail = tail.astype(F32)
    return tail[:, 0:1] + tail[:, 1:2] + tail[:, 2:3]


def merge(parts):
    top = functools.reduce(jnp.maximum, [s for _, s in parts])
    factors = [jnp.exp(s - top) for _, s in parts]
    total = functools.reduce(jnp.add, factors)
    mixed = functools.reduce(jnp.add, [f * o for f, (o, _) in zip(factors, parts)])
    return mixed / total, top + jnp.log(total)


def pair_kernel(latent, got_ref, keep_ref, sum_ref, after_ref, own_ref, own_sum_ref, *send_refs):
    for i in range(got_ref.shape[0]):
        got = got_ref[i]
        out, lse = merge(
            [
                (got[:, :latent].astype(F32), unpacked(got[:, latent:])),
                (keep_ref[i], sum_ref[i][:, 0:1]),
            ]
        )
        lse = jnp.broadcast_to(lse, (lse.shape[0], LANES))
        if i == 0:
            own_ref[...] = out
            own_sum_ref[...] = lse
        else:
            send_refs[i - 1][:, :latent] = out.astype(BF16)
            send_refs[i - 1][:, latent:] = packed(lse)


def value_kernel(latent, heads, own_ref, own_sum_ref, w_ref, *refs):
    got_refs, out_ref = refs[:-1], refs[-1]
    parts = [(own_ref[...], own_sum_ref[...][:, 0:1])]
    for got_ref in got_refs:
        got = got_ref[...]
        parts.append((got[:, :latent].astype(F32), unpacked(got[:, latent:])))
    mixed = merge(parts)[0].astype(BF16)
    size = w_ref.shape[2]
    head = lax.broadcasted_iota(jnp.int32, (mixed.shape[0], size), 0) % heads
    out = jnp.zeros((mixed.shape[0], size), F32)
    step = 2 if heads % 2 == 0 else 1
    for i in range(0, heads, step):
        weight = jnp.concatenate([w_ref[i + j] for j in range(step)], axis=1)
        both = jnp.dot(mixed, weight, preferred_element_type=F32)
        for j in range(step):
            out = jnp.where(head == i + j, both[:, j * size : (j + 1) * size], out)
    out_ref[...] = out.reshape(out_ref.shape).astype(BF16)


def largest_kernel(
    mine_ref, other_ref, lengths_hbm, after_ref, bounds_ref, lengths_ref, sem
):
    requests, groups, pages = bounds_ref.shape
    copy = pltpu.make_async_copy(lengths_hbm, lengths_ref, sem)
    copy.start()
    copy.wait()
    first = (
        lax.axis_index("seq") * pages + lax.broadcasted_iota(jnp.int32, (groups, pages), 1)
    ) * PAGE
    for r in range(requests):
        bounds_ref[r] = jnp.where(
            first < lengths_ref[r], jnp.maximum(mine_ref[r], other_ref[r]), 0.0
        )


def bounds_kernel(scale, heads, offsets, *refs):
    count = len(offsets)
    block_refs = refs[:count]
    low_ref, high_ref, after_ref, out_ref = refs[count:]
    requests, groups, pages = out_ref.shape
    blocks = [b[...].astype(F32) for b in block_refs]
    group = lax.broadcasted_iota(jnp.int32, (groups, pages), 0)
    dims = (((1,), (1,)), ((), ()))
    for r in range(requests):
        query = queries_of(blocks, r, heads)
        bound = lax.dot_general(
            jnp.maximum(query, 0.0).astype(BF16),
            high_ref[r].astype(BF16),
            dims,
            preferred_element_type=F32,
        ) + lax.dot_general(
            jnp.minimum(query, 0.0).astype(BF16),
            low_ref[r].astype(BF16),
            dims,
            preferred_element_type=F32,
        )
        bound = bound * scale
        best = jnp.full((groups, pages), NEG, F32)
        for i, k in enumerate(offsets):
            peak = jnp.max(bound[i * heads : (i + 1) * heads], axis=0, keepdims=True)
            best = jnp.where(group == group_of(k, heads), jnp.maximum(best, peak), best)
        out_ref[r] = best


def local(q_nope, q_rope, w_uk, w_uv, cache, lengths, selected):
    seq_count = lax.axis_size("seq")
    head_count = lax.axis_size("head")
    requests, heads, _ = q_nope.shape
    latent = w_uk.shape[2]
    width = cache.shape[2]
    tokens = cache.shape[1]
    pages = tokens // PAGE
    groups = selected.shape[1]
    rows = requests * heads
    scale = (q_nope.shape[2] + q_rope.shape[2]) ** (-0.5)
    assert seq_count & (seq_count - 1) == 0 and GH % heads == 0
    offsets = tuple(range(seq_count))
    far = tuple(reversed(range(2, seq_count, 2)))
    half = seq_count // 2
    slots = jnp.swapaxes(cache, 1, 2)

    q_nope, q_rope, w_uk, w_uv, slots, lengths, selected = (
        pltpu.with_memory_space_constraint(x, pltpu.HBM)
        for x in (q_nope, q_rope, w_uk, w_uv, slots, lengths, selected)
    )

    def swap(x, k):
        return lax.ppermute(x, "seq", [(i, i ^ k) for i in range(seq_count)])

    mine = pl.pallas_call(
        absorb_kernel,
        out_shape=jax.ShapeDtypeStruct((rows, width), BF16),
        in_specs=[HBM] * 3,
        out_specs=VMEM,
        scratch_shapes=[
            pltpu.VMEM(q_nope.shape, BF16),
            pltpu.VMEM(q_rope.shape, BF16),
            pltpu.VMEM(w_uk.shape, BF16),
            pltpu.SemaphoreType.DMA((heads + 2,)),
        ],
        compiler_params=params(),
        name="absorb",
    )(q_nope, q_rope, w_uk)
    block = {0: mine}
    for k in far:
        block[k] = swap(mine, k)
    block[1] = swap(mine, 1)
    for k in far:
        block[k + 1] = swap(block[k], 1)
    blocks = [block[k] for k in offsets]

    keys, w_value, mask, low, high = pl.pallas_call(
        stage_kernel,
        out_shape=(
            jax.ShapeDtypeStruct(slots.shape, BF16),
            jax.ShapeDtypeStruct(w_uv.shape, BF16),
            jax.ShapeDtypeStruct((requests * groups, tokens), F32),
            jax.ShapeDtypeStruct((requests, pages, width), F32),
            jax.ShapeDtypeStruct((requests, pages, width), F32),
        ),
        in_specs=[HBM] * 4 + [ANY],
        out_specs=(VMEM,) * 5,
        scratch_shapes=[
            pltpu.VMEM(selected.shape, jnp.int32),
            pltpu.SMEM(lengths.shape, jnp.int32),
            pltpu.SemaphoreType.DMA((3 + requests,)),
        ],
        compiler_params=params(),
        name="stage_cache",
    )(slots, w_uv, selected, lengths, block[far[-1]])

    send, keep, sums = pl.pallas_call(
        functools.partial(attend_kernel, scale, heads, offsets, latent),
        out_shape=(
            jax.ShapeDtypeStruct((half, rows, latent + LANES), BF16),
            jax.ShapeDtypeStruct((half, rows, latent), F32),
            jax.ShapeDtypeStruct((half, rows, LANES), F32),
        ),
        in_specs=[VMEM] * (seq_count + 2),
        out_specs=(VMEM,) * 3,
        compiler_params=params(),
        name="attend",
    )(*blocks, keys, mask)
    got = swap(send, 1)

    bounds = pl.pallas_call(
        functools.partial(bounds_kernel, scale, heads, offsets),
        out_shape=jax.ShapeDtypeStruct((requests, groups, pages), F32),
        in_specs=[VMEM] * (seq_count + 2) + [ANY],
        out_specs=VMEM,
        compiler_params=params(),
        name="page_bounds",
    )(*blocks, low, high, sums)
    others = lax.ppermute(
        bounds, "head", [(i, (i + 1) % head_count) for i in range(head_count)]
    )

    shape = jax.ShapeDtypeStruct((rows, latent + LANES), BF16)
    own, own_sum, *sends = pl.pallas_call(
        functools.partial(pair_kernel, latent),
        out_shape=(
            jax.ShapeDtypeStruct((rows, latent), F32),
            jax.ShapeDtypeStruct((rows, LANES), F32),
        )
        + (shape,) * (half - 1),
        in_specs=[VMEM] * 3 + [ANY],
        out_specs=(VMEM,) * (half + 1),
        compiler_params=params(),
        name="merge_pair",
    )(got, keep, sums, others)
    gots = {k: swap(sends[k // 2 - 1], k) for k in far}

    largest = pl.pallas_call(
        largest_kernel,
        out_shape=jax.ShapeDtypeStruct((requests, groups, pages), F32),
        in_specs=[VMEM] * 2 + [HBM, ANY],
        out_specs=VMEM,
        scratch_shapes=[pltpu.SMEM(lengths.shape, jnp.int32), pltpu.SemaphoreType.DMA(())],
        compiler_params=params(),
        name="group_bounds",
    )(bounds, others, lengths, own_sum)

    attended = pl.pallas_call(
        functools.partial(value_kernel, latent, heads),
        out_shape=jax.ShapeDtypeStruct((requests, heads, w_uv.shape[2]), BF16),
        in_specs=[VMEM] * (half + 2),
        out_specs=VMEM,
        compiler_params=params(),
        name="merge_and_value",
    )(own, own_sum, w_value, *[gots[k] for k in far])
    return attended, largest


def solution(mesh):
    assert mesh.shape["head"] == 2
    placed = (
        P("grp", ("seq", "head"), None),
        P("grp", ("seq", "head"), None),
        P(("seq", "head"), None, None),
        P(("seq", "head"), None, None),
        P("grp", "seq", None),
        P("grp"),
        P("grp", None, None),
    )
    return jax.shard_map(
        local,
        mesh=mesh,
        in_specs=placed,
        out_specs=(P("grp", ("seq", "head"), None), P("grp", None, "seq")),
        check_vma=False,
    )
```

```python
import functools

import jax
import jax.numpy as jnp
from jax import lax
from jax.experimental import pallas as pl
from jax.experimental.pallas import tpu as pltpu
from jax.sharding import PartitionSpec as P

GH = 16
PAGE = 64
NEG = -1e30
BF16 = jnp.bfloat16
F32 = jnp.float32
LANES = 128
VMEM = pl.BlockSpec(memory_space=pltpu.VMEM)
SMEM = pl.BlockSpec(memory_space=pltpu.SMEM)
HBM = pl.BlockSpec(memory_space=pltpu.HBM)
ANY = pl.BlockSpec(memory_space=pl.ANY)


def params(mib=24):
    return pltpu.CompilerParams(vmem_limit_bytes=mib << 20)


def absorb_kernel(nope_hbm, rope_hbm, w_hbm, out_ref, nope_ref, rope_ref, w_ref, sems):
    requests, heads, size = nope_ref.shape
    latent = w_ref.shape[2]
    rows = requests * heads
    step = 2 if heads % 2 == 0 else 1
    pieces = heads // step
    small = [
        pltpu.make_async_copy(nope_hbm, nope_ref, sems.at[pieces]),
        pltpu.make_async_copy(rope_hbm, rope_ref, sems.at[pieces + 1]),
    ]
    large = [
        pltpu.make_async_copy(
            w_hbm.at[pl.ds(i * step, step)], w_ref.at[pl.ds(i * step, step)], sems.at[i]
        )
        for i in range(pieces)
    ]
    for copy in small + large:
        copy.start()
    for copy in small:
        copy.wait()
    nope = nope_ref[...].astype(F32).reshape(rows, size)
    head = lax.broadcasted_iota(jnp.int32, (rows, size), 0) % heads
    out_ref[:, latent:] = rope_ref[...].astype(F32).reshape(rows, rope_ref.shape[2]).astype(BF16)
    total = jnp.zeros((rows, latent), F32)
    for i, copy in enumerate(large):
        wide = jnp.concatenate(
            [jnp.where(head == i * step + j, nope, 0.0) for j in range(step)], axis=1
        ).astype(BF16)
        copy.wait()
        weight = w_ref[i * step : (i + 1) * step].reshape(step * size, latent)
        total += jnp.dot(wide, weight, preferred_element_type=F32)
    out_ref[:, :latent] = total.astype(BF16)


def stage_kernel(
    cache_hbm, w_hbm, selected_hbm, lengths_hbm, after_ref,
    cache_ref, w_ref, mask_ref, low_ref, high_ref, live_ref, selected_ref, lengths_ref, sems,
):
    requests, groups, picks = selected_ref.shape
    width, tokens = cache_ref.shape[1:]
    pages = tokens // PAGE
    rank = lax.axis_index("seq")
    copies = [
        pltpu.make_async_copy(selected_hbm, selected_ref, sems.at[0]),
        pltpu.make_async_copy(lengths_hbm, lengths_ref, sems.at[1]),
        *(
            pltpu.make_async_copy(cache_hbm.at[r], cache_ref.at[r], sems.at[3 + r])
            for r in range(requests)
        ),
        pltpu.make_async_copy(w_hbm, w_ref, sems.at[2]),
    ]
    for copy in copies:
        copy.start()
    copies[0].wait()
    copies[1].wait()
    place = selected_ref[...].reshape(requests * groups, picks) - rank * pages
    here = (place >= 0) & (place < pages)
    bits = jnp.sum(
        jnp.where(here, jnp.left_shift(1, jnp.where(here, place, 0)), 0).astype(F32),
        axis=1,
        keepdims=True,
    ).astype(jnp.int32)
    lane = lax.broadcasted_iota(jnp.int32, (groups, tokens), 1)
    for r in range(requests):
        word = bits[r * groups : (r + 1) * groups]
        picked = jnp.bitwise_and(jnp.right_shift(word, lane // PAGE), 1) == 1
        live = lane + rank * tokens < lengths_ref[r]
        mask_ref[r * groups : (r + 1) * groups, :] = jnp.where(picked & live, 1.0, 0.0)
    first = (rank * pages + lax.broadcasted_iota(jnp.int32, (groups, pages), 1)) * PAGE
    row = lax.broadcasted_iota(jnp.int32, (tokens, width), 0) + rank * tokens
    for r in range(requests):
        live_ref[r] = jnp.where(first < lengths_ref[r], 1.0, 0.0)
        copies[2 + r].wait()
        slots = cache_ref[r].astype(F32).T
        live = row < lengths_ref[r]
        slots = slots.reshape(pages, PAGE, width)
        slots = jnp.where(live.reshape(pages, PAGE, width), slots, slots[:, 0:1, :])
        low_ref[r] = jnp.min(slots, axis=1)
        high_ref[r] = jnp.max(slots, axis=1)
    copies[-1].wait()


def split3(x):
    high = x.astype(BF16)
    rest = x - high.astype(F32)
    middle = rest.astype(BF16)
    return high, middle, (rest - middle.astype(F32)).astype(BF16)


def queries_of(blocks, request, heads):
    rows = slice(request * heads, (request + 1) * heads)
    return jnp.concatenate([b[rows] for b in blocks], axis=0)


def crossings(offset):
    return (1 if offset >> 1 else 0) + (offset & 1)


def group_of(offset, heads):
    source = jnp.bitwise_xor(lax.axis_index("seq"), offset)
    core = jnp.bitwise_xor(lax.axis_index("head"), crossings(offset) & 1)
    return (source * lax.axis_size("head") + core) * heads // GH


def attend_kernel(scale, heads, offsets, latent, *refs):
    count = len(offsets)
    block_refs = refs[:count]
    cache_ref, mask_ref, *out_refs = refs[count:]
    requests, _, tokens = cache_ref.shape
    groups = mask_ref.shape[0] // requests
    blocks = [b[...].astype(F32) for b in block_refs]
    outs, sums = [], []
    for r in range(requests):
        query = queries_of(blocks, r, heads).astype(BF16)
        keys = cache_ref[r]
        scores = jnp.dot(query, keys, preferred_element_type=F32) * scale
        mask = jnp.concatenate(
            [
                jnp.broadcast_to(
                    mask_ref[pl.ds(r * groups + group_of(k, heads), 1), :], (heads, tokens)
                )
                for k in offsets
            ],
            axis=0,
        )
        scores = jnp.where(mask > 0.5, scores, NEG)
        top = jnp.max(scores, axis=1, keepdims=True)
        weights = jnp.where(mask > 0.5, jnp.exp(scores - top), 0.0).astype(BF16)
        total = jnp.sum(weights.astype(F32), axis=1, keepdims=True)
        weighted = lax.dot_general(
            weights, keys[:latent], (((1,), (1,)), ((), ())), preferred_element_type=F32
        )
        some = total > 0.0
        safe = jnp.where(some, total, 1.0)
        outs.append(weighted / safe)
        sums.append(jnp.where(some, top + jnp.log(safe), NEG))
    for i, k in enumerate(offsets):
        rows = slice(i * heads, (i + 1) * heads)
        out = jnp.concatenate([o[rows] for o in outs], axis=0)
        lse = jnp.concatenate([s[rows] for s in sums], axis=0)
        fill(out_refs[i], out, lse)


def fill(ref, out, lse):
    latent = out.shape[1]
    lse = jnp.broadcast_to(lse, (lse.shape[0], LANES))
    ref[:, :latent] = out.astype(ref.dtype)
    ref[:, latent:] = packed(lse) if ref.dtype == BF16 else lse


def read(ref, latent):
    tail = ref[:, latent:].astype(F32)
    if ref.dtype == BF16:
        lse = tail[:, 0:1] + tail[:, 1:2] + tail[:, 2:3]
    else:
        lse = tail[:, 0:1]
    return ref[:, :latent].astype(F32), lse


def packed(lse):
    lane = lax.broadcasted_iota(jnp.int32, lse.shape, 1)
    high, middle, low = (p.astype(F32) for p in split3(lse))
    return jnp.where(lane == 0, high, jnp.where(lane == 1, middle, low)).astype(BF16)


def merge(parts):
    top = functools.reduce(jnp.maximum, [s for _, s in parts])
    factors = [jnp.exp(s - top) for _, s in parts]
    total = functools.reduce(jnp.add, factors)
    mixed = functools.reduce(jnp.add, [f * o for f, (o, _) in zip(factors, parts)])
    return mixed / total, top + jnp.log(total)


def pair_kernel(latent, got_ref, keep_ref, out_ref):
    fill(out_ref, *merge([read(got_ref, latent), read(keep_ref, latent)]))


def value_kernel(latent, heads, w_ref, *refs):
    part_refs, out_ref = refs[:-1], refs[-1]
    mixed = merge([read(ref, latent) for ref in part_refs])[0].astype(BF16)
    size = w_ref.shape[2]
    head = lax.broadcasted_iota(jnp.int32, (mixed.shape[0], size), 0) % heads
    out = jnp.zeros((mixed.shape[0], size), F32)
    step = 2 if heads % 2 == 0 else 1
    for i in range(0, heads, step):
        weight = jnp.concatenate([w_ref[i + j] for j in range(step)], axis=1)
        both = jnp.dot(mixed, weight, preferred_element_type=F32)
        for j in range(step):
            out = jnp.where(head == i + j, both[:, j * size : (j + 1) * size], out)
    out_ref[...] = out.reshape(out_ref.shape).astype(BF16)


def largest_kernel(mine_ref, other_ref, live_ref, bounds_ref):
    bounds_ref[...] = jnp.where(
        live_ref[...] > 0.5, jnp.maximum(mine_ref[...], other_ref[...]), 0.0
    )


def bounds_kernel(scale, heads, offsets, *refs):
    count = len(offsets)
    block_refs = refs[:count]
    low_ref, high_ref, after_ref, out_ref = refs[count:]
    requests, groups, pages = out_ref.shape
    blocks = [b[...].astype(F32) for b in block_refs]
    group = lax.broadcasted_iota(jnp.int32, (groups, pages), 0)
    dims = (((1,), (1,)), ((), ()))
    for r in range(requests):
        query = queries_of(blocks, r, heads)
        bound = lax.dot_general(
            jnp.maximum(query, 0.0).astype(BF16),
            high_ref[r].astype(BF16),
            dims,
            preferred_element_type=F32,
        ) + lax.dot_general(
            jnp.minimum(query, 0.0).astype(BF16),
            low_ref[r].astype(BF16),
            dims,
            preferred_element_type=F32,
        )
        bound = bound * scale
        best = jnp.full((groups, pages), NEG, F32)
        for i, k in enumerate(offsets):
            peak = jnp.max(bound[i * heads : (i + 1) * heads], axis=0, keepdims=True)
            best = jnp.where(group == group_of(k, heads), jnp.maximum(best, peak), best)
        out_ref[r] = best


def local(q_nope, q_rope, w_uk, w_uv, cache, lengths, selected):
    seq_count = lax.axis_size("seq")
    head_count = lax.axis_size("head")
    requests, heads, _ = q_nope.shape
    latent = w_uk.shape[2]
    width = cache.shape[2]
    tokens = cache.shape[1]
    pages = tokens // PAGE
    groups = selected.shape[1]
    rows = requests * heads
    scale = (q_nope.shape[2] + q_rope.shape[2]) ** (-0.5)
    assert seq_count & (seq_count - 1) == 0 and GH % heads == 0
    offsets = tuple(range(seq_count))
    far = tuple(reversed(range(2, seq_count, 2)))
    half = seq_count // 2
    slots = jnp.swapaxes(cache, 1, 2)

    q_nope, q_rope, w_uk, w_uv, slots, lengths, selected = (
        pltpu.with_memory_space_constraint(x, pltpu.HBM)
        for x in (q_nope, q_rope, w_uk, w_uv, slots, lengths, selected)
    )

    def swap(x, k):
        pairs = [
            (i * head_count + c, (i ^ k) * head_count + (c ^ 1))
            for i in range(seq_count)
            for c in range(head_count)
        ]
        return lax.ppermute(x, ("seq", "head"), pairs)

    mine = pl.pallas_call(
        absorb_kernel,
        out_shape=jax.ShapeDtypeStruct((rows, width), BF16),
        in_specs=[HBM] * 3,
        out_specs=VMEM,
        scratch_shapes=[
            pltpu.VMEM(q_nope.shape, BF16),
            pltpu.VMEM(q_rope.shape, BF16),
            pltpu.VMEM(w_uk.shape, BF16),
            pltpu.SemaphoreType.DMA((heads + 2,)),
        ],
        compiler_params=params(),
        name="absorb",
    )(q_nope, q_rope, w_uk)
    block = {0: mine}
    for k in far:
        block[k] = swap(mine, k)
    block[1] = swap(mine, 1)
    for k in far:
        block[k + 1] = swap(block[k], 1)
    blocks = [block[k] for k in offsets]

    keys, w_value, mask, low, high, live = pl.pallas_call(
        stage_kernel,
        out_shape=(
            jax.ShapeDtypeStruct(slots.shape, BF16),
            jax.ShapeDtypeStruct(w_uv.shape, BF16),
            jax.ShapeDtypeStruct((requests * groups, tokens), F32),
            jax.ShapeDtypeStruct((requests, pages, width), F32),
            jax.ShapeDtypeStruct((requests, pages, width), F32),
            jax.ShapeDtypeStruct((requests, groups, pages), F32),
        ),
        in_specs=[HBM] * 4 + [ANY],
        out_specs=(VMEM,) * 6,
        scratch_shapes=[
            pltpu.VMEM(selected.shape, jnp.int32),
            pltpu.SMEM(lengths.shape, jnp.int32),
            pltpu.SemaphoreType.DMA((3 + requests,)),
        ],
        compiler_params=params(),
        name="stage_cache",
    )(slots, w_uv, selected, lengths, block[far[-1]])

    parts = pl.pallas_call(
        functools.partial(attend_kernel, scale, heads, offsets, latent),
        out_shape=tuple(
            jax.ShapeDtypeStruct((rows, latent + LANES), BF16 if k % 2 else F32) for k in offsets
        ),
        in_specs=[VMEM] * (seq_count + 2),
        out_specs=(VMEM,) * seq_count,
        compiler_params=params(),
        name="attend",
    )(*blocks, keys, mask)

    got = {k: swap(parts[k + 1], 1) for k in far + (0,)}
    send = {
        k: pl.pallas_call(
            functools.partial(pair_kernel, latent),
            out_shape=jax.ShapeDtypeStruct((rows, latent + LANES), BF16),
            in_specs=[VMEM] * 2,
            out_specs=VMEM,
            compiler_params=params(),
            name="merge_pair",
        )(got[k], parts[k])
        for k in far
    }
    arrived = [swap(send[k], k) for k in far]

    bounds = pl.pallas_call(
        functools.partial(bounds_kernel, scale, heads, offsets),
        out_shape=jax.ShapeDtypeStruct((requests, groups, pages), F32),
        in_specs=[VMEM] * (seq_count + 2) + [ANY],
        out_specs=VMEM,
        compiler_params=params(),
        name="page_bounds",
    )(*blocks, low, high, send[far[-1]])
    others = lax.ppermute(bounds, "head", [(i, i ^ 1) for i in range(head_count)])
    largest = pl.pallas_call(
        largest_kernel,
        out_shape=jax.ShapeDtypeStruct((requests, groups, pages), F32),
        in_specs=[VMEM] * 3,
        out_specs=VMEM,
        compiler_params=params(),
        name="group_bounds",
    )(bounds, others, live)

    attended = pl.pallas_call(
        functools.partial(value_kernel, latent, heads),
        out_shape=jax.ShapeDtypeStruct((requests, heads, w_uv.shape[2]), BF16),
        in_specs=[VMEM] * (half + 2),
        out_specs=VMEM,
        compiler_params=params(),
        name="merge_and_value",
    )(w_value, parts[0], got[0], *arrived)
    return attended, largest


def solution(mesh):
    assert mesh.shape["head"] == 2
    placed = (
        P("grp", ("seq", "head"), None),
        P("grp", ("seq", "head"), None),
        P(("seq", "head"), None, None),
        P(("seq", "head"), None, None),
        P("grp", "seq", None),
        P("grp"),
        P("grp", None, None),
    )
    return jax.shard_map(
        local,
        mesh=mesh,
        in_specs=placed,
        out_specs=(P("grp", ("seq", "head"), None), P("grp", None, "seq")),
        check_vma=False,
    )
```

```python
import functools

import jax
import jax.numpy as jnp
from jax import lax
from jax.experimental import pallas as pl
from jax.experimental.pallas import tpu as pltpu
from jax.sharding import PartitionSpec as P

GH = 16
PAGE = 64
NEG = -1e30
BF16 = jnp.bfloat16
F32 = jnp.float32
LANES = 128
LOG2E = 1.4426950408889634
VMEM = pl.BlockSpec(memory_space=pltpu.VMEM)
SMEM = pl.BlockSpec(memory_space=pltpu.SMEM)
HBM = pl.BlockSpec(memory_space=pltpu.HBM)
ANY = pl.BlockSpec(memory_space=pl.ANY)


def params(mib=24):
    return pltpu.CompilerParams(vmem_limit_bytes=mib << 20)


def absorb_kernel(nope_hbm, rope_hbm, w_hbm, out_ref, nope_ref, rope_ref, w_ref, sems):
    requests, heads, size = nope_ref.shape
    latent = w_ref.shape[2]
    rows = requests * heads
    step = 2 if heads % 2 == 0 else 1
    pieces = heads // step
    small = [
        pltpu.make_async_copy(nope_hbm, nope_ref, sems.at[pieces]),
        pltpu.make_async_copy(rope_hbm, rope_ref, sems.at[pieces + 1]),
    ]
    large = [
        pltpu.make_async_copy(
            w_hbm.at[pl.ds(i * step, step)], w_ref.at[pl.ds(i * step, step)], sems.at[i]
        )
        for i in range(pieces)
    ]
    for copy in small + large:
        copy.start()
    for copy in small:
        copy.wait()
    nope = nope_ref[...].astype(F32).reshape(rows, size)
    head = lax.broadcasted_iota(jnp.int32, (rows, size), 0) % heads
    out_ref[:, latent:] = rope_ref[...].astype(F32).reshape(rows, rope_ref.shape[2]).astype(BF16)
    total = jnp.zeros((rows, latent), F32)
    for i, copy in enumerate(large):
        wide = jnp.concatenate(
            [jnp.where(head == i * step + j, nope, 0.0) for j in range(step)], axis=1
        ).astype(BF16)
        copy.wait()
        weight = w_ref[i * step : (i + 1) * step].reshape(step * size, latent)
        total += jnp.dot(wide, weight, preferred_element_type=F32)
    out_ref[:, :latent] = total.astype(BF16)


def stage_kernel(
    cache_hbm, selected_hbm, lengths_hbm, after_ref,
    cache_ref, slots_ref, mask_ref, low_ref, high_ref, live_ref, selected_ref, lengths_ref, sems,
):
    requests, groups, picks = selected_ref.shape
    width, tokens = cache_ref.shape[1:]
    pages = tokens // PAGE
    rank = lax.axis_index("seq")
    copies = [
        pltpu.make_async_copy(selected_hbm, selected_ref, sems.at[0]),
        pltpu.make_async_copy(lengths_hbm, lengths_ref, sems.at[1]),
        *(
            pltpu.make_async_copy(cache_hbm.at[r], cache_ref.at[r], sems.at[2 + r])
            for r in range(requests)
        ),
    ]
    for copy in copies:
        copy.start()
    copies[0].wait()
    copies[1].wait()
    place = selected_ref[...].reshape(requests * groups, picks) - rank * pages
    here = (place >= 0) & (place < pages)
    bits = jnp.sum(
        jnp.where(here, jnp.left_shift(1, jnp.where(here, place, 0)), 0).astype(F32),
        axis=1,
        keepdims=True,
    ).astype(jnp.int32)
    lane = lax.broadcasted_iota(jnp.int32, (groups, tokens), 1)
    for r in range(requests):
        word = bits[r * groups : (r + 1) * groups]
        picked = jnp.bitwise_and(jnp.right_shift(word, lane // PAGE), 1) == 1
        live = lane + rank * tokens < lengths_ref[r]
        mask_ref[r * groups : (r + 1) * groups, :] = jnp.where(picked & live, 1.0, 0.0)
    first = (rank * pages + lax.broadcasted_iota(jnp.int32, (groups, pages), 1)) * PAGE
    row = lax.broadcasted_iota(jnp.int32, (tokens, width), 0) + rank * tokens
    for r in range(requests):
        live_ref[r] = jnp.where(first < lengths_ref[r], 1.0, 0.0)
        copies[2 + r].wait()
        slots = cache_ref[r].T
        slots_ref[r] = slots[:, : slots_ref.shape[2]]
        slots = slots.astype(F32)
        live = row < lengths_ref[r]
        slots = slots.reshape(pages, PAGE, width)
        slots = jnp.where(live.reshape(pages, PAGE, width), slots, slots[:, 0:1, :])
        low_ref[r] = jnp.min(slots, axis=1)
        high_ref[r] = jnp.max(slots, axis=1)


def split3(x):
    high = x.astype(BF16)
    rest = x - high.astype(F32)
    middle = rest.astype(BF16)
    return high, middle, (rest - middle.astype(F32)).astype(BF16)


def queries_of(blocks, request, heads):
    rows = slice(request * heads, (request + 1) * heads)
    return jnp.concatenate([b[rows] for b in blocks], axis=0)


def crossings(offset):
    return (1 if offset >> 1 else 0) + (offset & 1)


def group_of(offset, heads):
    source = jnp.bitwise_xor(lax.axis_index("seq"), offset)
    core = jnp.bitwise_xor(lax.axis_index("head"), crossings(offset) & 1)
    return (source * lax.axis_size("head") + core) * heads // GH


def attend_kernel(scale, heads, offsets, latent, *refs):
    count = len(offsets)
    block_refs = refs[:count]
    cache_ref, slots_ref, mask_ref, *out_refs = refs[count:]
    requests, _, tokens = cache_ref.shape
    groups = mask_ref.shape[0] // requests
    blocks = [b[...].astype(F32) for b in block_refs]
    outs, sums = [], []
    for r in range(requests):
        query = queries_of(blocks, r, heads).astype(BF16)
        keys = cache_ref[r]
        scores = jnp.dot(query, keys, preferred_element_type=F32)
        mask = jnp.concatenate(
            [
                jnp.broadcast_to(
                    mask_ref[pl.ds(r * groups + group_of(k, heads), 1), :], (heads, tokens)
                )
                for k in offsets
            ],
            axis=0,
        )
        scores = jnp.where(mask > 0.5, scores, NEG)
        top = jnp.max(scores, axis=1, keepdims=True)
        weights = jnp.exp2((scores - top) * (scale * LOG2E)).astype(BF16)
        total = jnp.sum(weights.astype(F32), axis=1, keepdims=True)
        weighted = jnp.dot(weights, slots_ref[r], preferred_element_type=F32)
        outs.append(weighted * (1.0 / total))
        sums.append(top * scale + jnp.log(total))
    for i, k in enumerate(offsets):
        rows = slice(i * heads, (i + 1) * heads)
        out = jnp.concatenate([o[rows] for o in outs], axis=0)
        lse = jnp.concatenate([s[rows] for s in sums], axis=0)
        fill(out_refs[i], out, lse)


def fill(ref, out, lse):
    latent = out.shape[1]
    lse = jnp.broadcast_to(lse, (lse.shape[0], LANES))
    ref[:, :latent] = out.astype(ref.dtype)
    ref[:, latent:] = packed(lse) if ref.dtype == BF16 else lse


def read(ref, latent):
    tail = ref[:, latent:].astype(F32)
    if ref.dtype == BF16:
        lse = tail[:, 0:1] + tail[:, 1:2] + tail[:, 2:3]
    else:
        lse = tail[:, 0:1]
    return ref[:, :latent].astype(F32), lse


def packed(lse):
    lane = lax.broadcasted_iota(jnp.int32, lse.shape, 1)
    high, middle, low = (p.astype(F32) for p in split3(lse))
    return jnp.where(lane == 0, high, jnp.where(lane == 1, middle, low)).astype(BF16)


def merge(parts):
    top = functools.reduce(jnp.maximum, [s for _, s in parts])
    factors = [jnp.exp(s - top) for _, s in parts]
    total = functools.reduce(jnp.add, factors)
    mixed = functools.reduce(jnp.add, [f * o for f, (o, _) in zip(factors, parts)])
    return mixed / total, top + jnp.log(total)


def pair_kernel(latent, got_ref, keep_ref, out_ref):
    fill(out_ref, *merge([read(got_ref, latent), read(keep_ref, latent)]))


def value_kernel(latent, heads, w_ref, *refs):
    part_refs, out_ref = refs[:-1], refs[-1]
    mixed = merge([read(ref, latent) for ref in part_refs])[0].astype(BF16)
    size = w_ref.shape[2]
    head = lax.broadcasted_iota(jnp.int32, (mixed.shape[0], size), 0) % heads
    out = jnp.zeros((mixed.shape[0], size), F32)
    step = 2 if heads % 2 == 0 else 1
    for i in range(0, heads, step):
        weight = jnp.concatenate([w_ref[i + j] for j in range(step)], axis=1)
        both = jnp.dot(mixed, weight, preferred_element_type=F32)
        for j in range(step):
            out = jnp.where(head == i + j, both[:, j * size : (j + 1) * size], out)
    out_ref[...] = out.reshape(out_ref.shape).astype(BF16)


def largest_kernel(mine_ref, other_ref, live_ref, bounds_ref):
    bounds_ref[...] = jnp.where(
        live_ref[...] > 0.5, jnp.maximum(mine_ref[...], other_ref[...]), 0.0
    )


def bounds_kernel(scale, heads, offsets, *refs):
    count = len(offsets)
    block_refs = refs[:count]
    low_ref, high_ref, after_ref, out_ref = refs[count:]
    requests, groups, pages = out_ref.shape
    blocks = [b[...].astype(F32) for b in block_refs]
    group = lax.broadcasted_iota(jnp.int32, (groups, pages), 0)
    dims = (((1,), (1,)), ((), ()))
    for r in range(requests):
        query = queries_of(blocks, r, heads)
        bound = lax.dot_general(
            jnp.maximum(query, 0.0).astype(BF16),
            high_ref[r].astype(BF16),
            dims,
            preferred_element_type=F32,
        ) + lax.dot_general(
            jnp.minimum(query, 0.0).astype(BF16),
            low_ref[r].astype(BF16),
            dims,
            preferred_element_type=F32,
        )
        bound = bound * scale
        best = jnp.full((groups, pages), NEG, F32)
        for i, k in enumerate(offsets):
            peak = jnp.max(bound[i * heads : (i + 1) * heads], axis=0, keepdims=True)
            best = jnp.where(group == group_of(k, heads), jnp.maximum(best, peak), best)
        out_ref[r] = best


def local(q_nope, q_rope, w_uk, w_uv, cache, lengths, selected):
    seq_count = lax.axis_size("seq")
    head_count = lax.axis_size("head")
    requests, heads, _ = q_nope.shape
    latent = w_uk.shape[2]
    width = cache.shape[2]
    tokens = cache.shape[1]
    pages = tokens // PAGE
    groups = selected.shape[1]
    rows = requests * heads
    scale = (q_nope.shape[2] + q_rope.shape[2]) ** (-0.5)
    assert seq_count & (seq_count - 1) == 0 and GH % heads == 0
    offsets = tuple(range(seq_count))
    far = tuple(reversed(range(2, seq_count, 2)))
    half = seq_count // 2
    slots = jnp.swapaxes(cache, 1, 2)

    q_nope, q_rope, w_uk, slots, lengths, selected = (
        pltpu.with_memory_space_constraint(x, pltpu.HBM)
        for x in (q_nope, q_rope, w_uk, slots, lengths, selected)
    )

    def swap(x, k, flip=1):
        pairs = [
            (i * head_count + c, (i ^ k) * head_count + (c ^ flip))
            for i in range(seq_count)
            for c in range(head_count)
        ]
        return lax.ppermute(x, ("seq", "head"), pairs)

    mine = pl.pallas_call(
        absorb_kernel,
        out_shape=jax.ShapeDtypeStruct((rows, width), BF16),
        in_specs=[HBM] * 3,
        out_specs=VMEM,
        scratch_shapes=[
            pltpu.VMEM(q_nope.shape, BF16),
            pltpu.VMEM(q_rope.shape, BF16),
            pltpu.VMEM(w_uk.shape, BF16),
            pltpu.SemaphoreType.DMA((heads + 2,)),
        ],
        compiler_params=params(),
        name="absorb",
    )(q_nope, q_rope, w_uk)
    block = {0: mine}
    for k in far:
        block[k] = swap(mine, k)
    near = far[-1]
    block[near + 1] = swap(mine, near + 1, 0)
    block[1] = swap(mine, 1)
    for k in far[:-1]:
        block[k + 1] = swap(block[k], 1)
    blocks = [block[k] for k in offsets]

    keys, values, mask, low, high, live = pl.pallas_call(
        stage_kernel,
        out_shape=(
            jax.ShapeDtypeStruct(slots.shape, BF16),
            jax.ShapeDtypeStruct((requests, tokens, latent), BF16),
            jax.ShapeDtypeStruct((requests * groups, tokens), F32),
            jax.ShapeDtypeStruct((requests, pages, width), F32),
            jax.ShapeDtypeStruct((requests, pages, width), F32),
            jax.ShapeDtypeStruct((requests, groups, pages), F32),
        ),
        in_specs=[HBM] * 3 + [ANY],
        out_specs=(VMEM,) * 6,
        scratch_shapes=[
            pltpu.VMEM(selected.shape, jnp.int32),
            pltpu.SMEM(lengths.shape, jnp.int32),
            pltpu.SemaphoreType.DMA((2 + requests,)),
        ],
        compiler_params=params(),
        name="stage_cache",
    )(slots, selected, lengths, block[near])

    parts = pl.pallas_call(
        functools.partial(attend_kernel, scale, heads, offsets, latent),
        out_shape=tuple(
            jax.ShapeDtypeStruct((rows, latent + LANES), BF16 if k % 2 else F32) for k in offsets
        ),
        in_specs=[VMEM] * (seq_count + 3),
        out_specs=(VMEM,) * seq_count,
        compiler_params=params(),
        name="attend",
    )(*blocks, keys, values, mask)

    got = {k: swap(parts[k + 1], 1) for k in far + (0,)}
    send = {
        k: pl.pallas_call(
            functools.partial(pair_kernel, latent),
            out_shape=jax.ShapeDtypeStruct((rows, latent + LANES), BF16),
            in_specs=[VMEM] * 2,
            out_specs=VMEM,
            compiler_params=params(),
            name="merge_pair",
        )(got[k], parts[k])
        for k in far
    }
    arrived = [swap(send[k], k) for k in far]

    bounds = pl.pallas_call(
        functools.partial(bounds_kernel, scale, heads, offsets),
        out_shape=jax.ShapeDtypeStruct((requests, groups, pages), F32),
        in_specs=[VMEM] * (seq_count + 2) + [ANY],
        out_specs=VMEM,
        compiler_params=params(),
        name="page_bounds",
    )(*blocks, low, high, send[far[-1]])
    others = lax.ppermute(bounds, "head", [(i, i ^ 1) for i in range(head_count)])
    largest = pl.pallas_call(
        largest_kernel,
        out_shape=jax.ShapeDtypeStruct((requests, groups, pages), F32),
        in_specs=[VMEM] * 3,
        out_specs=VMEM,
        compiler_params=params(),
        name="group_bounds",
    )(bounds, others, live)

    attended = pl.pallas_call(
        functools.partial(value_kernel, latent, heads),
        out_shape=jax.ShapeDtypeStruct((requests, heads, w_uv.shape[2]), BF16),
        in_specs=[VMEM] * (half + 2),
        out_specs=VMEM,
        compiler_params=params(),
        name="merge_and_value",
    )(w_uv, parts[0], got[0], *arrived)
    return attended, largest


def solution(mesh):
    assert mesh.shape["head"] == 2
    placed = (
        P("grp", ("seq", "head"), None),
        P("grp", ("seq", "head"), None),
        P(("seq", "head"), None, None),
        P(("seq", "head"), None, None),
        P("grp", "seq", None),
        P("grp"),
        P("grp", None, None),
    )
    return jax.shard_map(
        local,
        mesh=mesh,
        in_specs=placed,
        out_specs=(P("grp", ("seq", "head"), None), P("grp", None, "seq")),
        check_vma=False,
    )
```

```python
import functools

import jax
import jax.numpy as jnp
from jax import lax
from jax.experimental import pallas as pl
from jax.experimental.pallas import tpu as pltpu
from jax.sharding import PartitionSpec as P

GH = 16
PAGE = 64
NEG = -1e30
BF16 = jnp.bfloat16
F32 = jnp.float32
LANES = 128
LOG2E = 1.4426950408889634
VMEM = pl.BlockSpec(memory_space=pltpu.VMEM)
SMEM = pl.BlockSpec(memory_space=pltpu.SMEM)
HBM = pl.BlockSpec(memory_space=pltpu.HBM)
ANY = pl.BlockSpec(memory_space=pl.ANY)


def params(mib=24):
    return pltpu.CompilerParams(vmem_limit_bytes=mib << 20)


def absorb_kernel(nope_hbm, rope_hbm, w_hbm, out_ref, nope_ref, rope_ref, w_ref, sems):
    requests, heads, size = nope_ref.shape
    latent = w_ref.shape[2]
    rows = requests * heads
    step = 2 if heads % 2 == 0 else 1
    pieces = heads // step
    small = [
        pltpu.make_async_copy(nope_hbm, nope_ref, sems.at[pieces]),
        pltpu.make_async_copy(rope_hbm, rope_ref, sems.at[pieces + 1]),
    ]
    large = [
        pltpu.make_async_copy(
            w_hbm.at[pl.ds(i * step, step)], w_ref.at[pl.ds(i * step, step)], sems.at[i]
        )
        for i in range(pieces)
    ]
    for copy in small + large:
        copy.start()
    for copy in small:
        copy.wait()
    nope = nope_ref[...].astype(F32).reshape(rows, size)
    head = lax.broadcasted_iota(jnp.int32, (rows, size), 0) % heads
    out_ref[:, latent:] = rope_ref[...].astype(F32).reshape(rows, rope_ref.shape[2]).astype(BF16)
    total = jnp.zeros((rows, latent), F32)
    for i, copy in enumerate(large):
        wide = jnp.concatenate(
            [jnp.where(head == i * step + j, nope, 0.0) for j in range(step)], axis=1
        ).astype(BF16)
        copy.wait()
        weight = w_ref[i * step : (i + 1) * step].reshape(step * size, latent)
        total += jnp.dot(wide, weight, preferred_element_type=F32)
    out_ref[:, :latent] = total.astype(BF16)


def stage_kernel(
    cache_hbm, selected_hbm, lengths_hbm, after_ref,
    cache_ref, slots_ref, mask_ref, low_ref, high_ref, live_ref, selected_ref, lengths_ref, sems,
):
    requests, groups, picks = selected_ref.shape
    width, tokens = cache_ref.shape[1:]
    pages = tokens // PAGE
    rank = lax.axis_index("seq")
    copies = [
        pltpu.make_async_copy(selected_hbm, selected_ref, sems.at[0]),
        pltpu.make_async_copy(lengths_hbm, lengths_ref, sems.at[1]),
        *(
            pltpu.make_async_copy(cache_hbm.at[r], cache_ref.at[r], sems.at[2 + r])
            for r in range(requests)
        ),
    ]
    for copy in copies:
        copy.start()
    copies[0].wait()
    copies[1].wait()
    place = selected_ref[...].reshape(requests * groups, picks) - rank * pages
    here = (place >= 0) & (place < pages)
    bits = jnp.sum(
        jnp.where(here, jnp.left_shift(1, jnp.where(here, place, 0)), 0).astype(F32),
        axis=1,
        keepdims=True,
    ).astype(jnp.int32)
    lane = lax.broadcasted_iota(jnp.int32, (groups, tokens), 1)
    for r in range(requests):
        word = bits[r * groups : (r + 1) * groups]
        picked = jnp.bitwise_and(jnp.right_shift(word, lane // PAGE), 1) == 1
        live = lane + rank * tokens < lengths_ref[r]
        mask_ref[r * groups : (r + 1) * groups, :] = jnp.where(picked & live, 1.0, 0.0)
    first = (rank * pages + lax.broadcasted_iota(jnp.int32, (groups, pages), 1)) * PAGE
    row = lax.broadcasted_iota(jnp.int32, (tokens, width), 0) + rank * tokens
    for r in range(requests):
        live_ref[r] = jnp.where(first < lengths_ref[r], 1.0, 0.0)
        copies[2 + r].wait()
        slots = cache_ref[r].T
        slots_ref[r] = slots[:, : slots_ref.shape[2]]
        slots = slots.astype(F32)
        live = row < lengths_ref[r]
        slots = slots.reshape(pages, PAGE, width)
        slots = jnp.where(live.reshape(pages, PAGE, width), slots, slots[:, 0:1, :])
        low_ref[r] = jnp.min(slots, axis=1)
        high_ref[r] = jnp.max(slots, axis=1)


def split3(x):
    high = x.astype(BF16)
    rest = x - high.astype(F32)
    middle = rest.astype(BF16)
    return high, middle, (rest - middle.astype(F32)).astype(BF16)


def queries_of(blocks, request, heads):
    rows = slice(request * heads, (request + 1) * heads)
    return jnp.concatenate([b[rows] for b in blocks], axis=0)


def crossings(offset):
    return (1 if offset >> 1 else 0) + (offset & 1)


def group_of(offset, heads):
    source = jnp.bitwise_xor(lax.axis_index("seq"), offset)
    core = jnp.bitwise_xor(lax.axis_index("head"), crossings(offset) & 1)
    return (source * lax.axis_size("head") + core) * heads // GH


def attend_kernel(scale, heads, offsets, latent, *refs):
    count = len(offsets)
    block_refs = refs[:count]
    cache_ref, slots_ref, mask_ref, *out_refs = refs[count:]
    requests, _, tokens = cache_ref.shape
    groups = mask_ref.shape[0] // requests
    blocks = [b[...].astype(F32) for b in block_refs]
    scores = [
        jnp.dot(
            queries_of(blocks, r, heads).astype(BF16), cache_ref[r], preferred_element_type=F32
        )
        for r in range(requests)
    ]
    weights, shares, sums = [], [], []
    for r in range(requests):
        mask = jnp.concatenate(
            [
                jnp.broadcast_to(
                    mask_ref[pl.ds(r * groups + group_of(k, heads), 1), :], (heads, tokens)
                )
                for k in offsets
            ],
            axis=0,
        )
        masked = jnp.where(mask > 0.5, scores[r], NEG)
        top = jnp.max(masked, axis=1, keepdims=True)
        weight = jnp.exp2((masked - top) * (scale * LOG2E)).astype(BF16)
        total = jnp.sum(weight.astype(F32), axis=1, keepdims=True)
        weights.append(weight)
        shares.append(1.0 / total)
        sums.append(top * scale + jnp.log(total))
    outs = [
        jnp.dot(weights[r], slots_ref[r], preferred_element_type=F32) * shares[r]
        for r in range(requests)
    ]
    for i, k in enumerate(offsets):
        rows = slice(i * heads, (i + 1) * heads)
        out = jnp.concatenate([o[rows] for o in outs], axis=0)
        lse = jnp.concatenate([s[rows] for s in sums], axis=0)
        fill(out_refs[i], out, lse)


def fill(ref, out, lse):
    latent = out.shape[1]
    lse = jnp.broadcast_to(lse, (lse.shape[0], LANES))
    ref[:, :latent] = out.astype(ref.dtype)
    ref[:, latent:] = packed(lse) if ref.dtype == BF16 else lse


def read(ref, latent):
    tail = ref[:, latent:].astype(F32)
    if ref.dtype == BF16:
        lse = tail[:, 0:1] + tail[:, 1:2] + tail[:, 2:3]
    else:
        lse = tail[:, 0:1]
    return ref[:, :latent].astype(F32), lse


def packed(lse):
    lane = lax.broadcasted_iota(jnp.int32, lse.shape, 1)
    high, middle, low = (p.astype(F32) for p in split3(lse))
    return jnp.where(lane == 0, high, jnp.where(lane == 1, middle, low)).astype(BF16)


def merge(parts):
    top = functools.reduce(jnp.maximum, [s for _, s in parts])
    factors = [jnp.exp(s - top) for _, s in parts]
    total = functools.reduce(jnp.add, factors)
    mixed = functools.reduce(jnp.add, [f * o for f, (o, _) in zip(factors, parts)])
    return mixed / total, top + jnp.log(total)


def pair_kernel(latent, got_ref, keep_ref, out_ref):
    fill(out_ref, *merge([read(got_ref, latent), read(keep_ref, latent)]))


def value_kernel(latent, heads, w_ref, *refs):
    part_refs, out_ref = refs[:-1], refs[-1]
    mixed = merge([read(ref, latent) for ref in part_refs])[0].astype(BF16)
    size = w_ref.shape[2]
    head = lax.broadcasted_iota(jnp.int32, (mixed.shape[0], size), 0) % heads
    out = jnp.zeros((mixed.shape[0], size), F32)
    step = 2 if heads % 2 == 0 else 1
    for i in range(0, heads, step):
        weight = jnp.concatenate([w_ref[i + j] for j in range(step)], axis=1)
        both = jnp.dot(mixed, weight, preferred_element_type=F32)
        for j in range(step):
            out = jnp.where(head == i + j, both[:, j * size : (j + 1) * size], out)
    out_ref[...] = out.reshape(out_ref.shape).astype(BF16)


def largest_kernel(mine_ref, other_ref, live_ref, bounds_ref):
    bounds_ref[...] = jnp.where(
        live_ref[...] > 0.5, jnp.maximum(mine_ref[...], other_ref[...]), 0.0
    )


def bounds_kernel(scale, heads, offsets, *refs):
    count = len(offsets)
    block_refs = refs[:count]
    low_ref, high_ref, after_ref, out_ref = refs[count:]
    requests, groups, pages = out_ref.shape
    blocks = [b[...].astype(F32) for b in block_refs]
    group = lax.broadcasted_iota(jnp.int32, (groups, pages), 0)
    dims = (((1,), (1,)), ((), ()))
    for r in range(requests):
        query = queries_of(blocks, r, heads)
        bound = lax.dot_general(
            jnp.maximum(query, 0.0).astype(BF16),
            high_ref[r].astype(BF16),
            dims,
            preferred_element_type=F32,
        ) + lax.dot_general(
            jnp.minimum(query, 0.0).astype(BF16),
            low_ref[r].astype(BF16),
            dims,
            preferred_element_type=F32,
        )
        bound = bound * scale
        best = jnp.full((groups, pages), NEG, F32)
        for i, k in enumerate(offsets):
            peak = jnp.max(bound[i * heads : (i + 1) * heads], axis=0, keepdims=True)
            best = jnp.where(group == group_of(k, heads), jnp.maximum(best, peak), best)
        out_ref[r] = best


def local(q_nope, q_rope, w_uk, w_uv, cache, lengths, selected):
    seq_count = lax.axis_size("seq")
    head_count = lax.axis_size("head")
    requests, heads, _ = q_nope.shape
    latent = w_uk.shape[2]
    width = cache.shape[2]
    tokens = cache.shape[1]
    pages = tokens // PAGE
    groups = selected.shape[1]
    rows = requests * heads
    scale = (q_nope.shape[2] + q_rope.shape[2]) ** (-0.5)
    assert seq_count & (seq_count - 1) == 0 and GH % heads == 0
    offsets = tuple(range(seq_count))
    far = tuple(reversed(range(2, seq_count, 2)))
    half = seq_count // 2
    slots = jnp.swapaxes(cache, 1, 2)

    q_nope, q_rope, w_uk, slots, lengths, selected = (
        pltpu.with_memory_space_constraint(x, pltpu.HBM)
        for x in (q_nope, q_rope, w_uk, slots, lengths, selected)
    )

    def swap(x, k, flip=1):
        pairs = [
            (i * head_count + c, (i ^ k) * head_count + (c ^ flip))
            for i in range(seq_count)
            for c in range(head_count)
        ]
        return lax.ppermute(x, ("seq", "head"), pairs)

    mine = pl.pallas_call(
        absorb_kernel,
        out_shape=jax.ShapeDtypeStruct((rows, width), BF16),
        in_specs=[HBM] * 3,
        out_specs=VMEM,
        scratch_shapes=[
            pltpu.VMEM(q_nope.shape, BF16),
            pltpu.VMEM(q_rope.shape, BF16),
            pltpu.VMEM(w_uk.shape, BF16),
            pltpu.SemaphoreType.DMA((heads + 2,)),
        ],
        compiler_params=params(),
        name="absorb",
    )(q_nope, q_rope, w_uk)
    block = {0: mine}
    for k in far:
        block[k] = swap(mine, k)
    near = far[-1]
    block[near + 1] = swap(mine, near + 1, 0)
    block[1] = swap(mine, 1)
    for k in far[:-1]:
        block[k + 1] = swap(block[k], 1)
    blocks = [block[k] for k in offsets]

    keys, values, mask, low, high, live = pl.pallas_call(
        stage_kernel,
        out_shape=(
            jax.ShapeDtypeStruct(slots.shape, BF16),
            jax.ShapeDtypeStruct((requests, tokens, latent), BF16),
            jax.ShapeDtypeStruct((requests * groups, tokens), F32),
            jax.ShapeDtypeStruct((requests, pages, width), F32),
            jax.ShapeDtypeStruct((requests, pages, width), F32),
            jax.ShapeDtypeStruct((requests, groups, pages), F32),
        ),
        in_specs=[HBM] * 3 + [ANY],
        out_specs=(VMEM,) * 6,
        scratch_shapes=[
            pltpu.VMEM(selected.shape, jnp.int32),
            pltpu.SMEM(lengths.shape, jnp.int32),
            pltpu.SemaphoreType.DMA((2 + requests,)),
        ],
        compiler_params=params(),
        name="stage_cache",
    )(slots, selected, lengths, block[near])

    parts = pl.pallas_call(
        functools.partial(attend_kernel, scale, heads, offsets, latent),
        out_shape=tuple(
            jax.ShapeDtypeStruct((rows, latent + LANES), BF16 if k % 2 else F32) for k in offsets
        ),
        in_specs=[VMEM] * (seq_count + 3),
        out_specs=(VMEM,) * seq_count,
        compiler_params=params(),
        name="attend",
    )(*blocks, keys, values, mask)

    got = {k: swap(parts[k + 1], 1) for k in far + (0,)}
    send = {
        k: pl.pallas_call(
            functools.partial(pair_kernel, latent),
            out_shape=jax.ShapeDtypeStruct((rows, latent + LANES), BF16),
            in_specs=[VMEM] * 2,
            out_specs=VMEM,
            compiler_params=params(),
            name="merge_pair",
        )(got[k], parts[k])
        for k in far
    }
    arrived = [swap(send[k], k) for k in far]

    bounds = pl.pallas_call(
        functools.partial(bounds_kernel, scale, heads, offsets),
        out_shape=jax.ShapeDtypeStruct((requests, groups, pages), F32),
        in_specs=[VMEM] * (seq_count + 2) + [ANY],
        out_specs=VMEM,
        compiler_params=params(),
        name="page_bounds",
    )(*blocks, low, high, send[far[-1]])
    others = lax.ppermute(bounds, "head", [(i, i ^ 1) for i in range(head_count)])
    largest = pl.pallas_call(
        largest_kernel,
        out_shape=jax.ShapeDtypeStruct((requests, groups, pages), F32),
        in_specs=[VMEM] * 3,
        out_specs=VMEM,
        compiler_params=params(),
        name="group_bounds",
    )(bounds, others, live)

    attended = pl.pallas_call(
        functools.partial(value_kernel, latent, heads),
        out_shape=jax.ShapeDtypeStruct((requests, heads, w_uv.shape[2]), BF16),
        in_specs=[VMEM] * (half + 2),
        out_specs=VMEM,
        compiler_params=params(),
        name="merge_and_value",
    )(w_uv, parts[0], got[0], *arrived)
    return attended, largest


def solution(mesh):
    assert mesh.shape["head"] == 2
    placed = (
        P("grp", ("seq", "head"), None),
        P("grp", ("seq", "head"), None),
        P(("seq", "head"), None, None),
        P(("seq", "head"), None, None),
        P("grp", "seq", None),
        P("grp"),
        P("grp", None, None),
    )
    return jax.shard_map(
        local,
        mesh=mesh,
        in_specs=placed,
        out_specs=(P("grp", ("seq", "head"), None), P("grp", None, "seq")),
        check_vma=False,
    )
```

```python
import functools

import jax
import jax.numpy as jnp
from jax import lax
from jax.experimental import pallas as pl
from jax.experimental.pallas import tpu as pltpu
from jax.sharding import PartitionSpec as P

GH = 16
PAGE = 64
NEG = -1e30
BF16 = jnp.bfloat16
F32 = jnp.float32
LANES = 128
LOG2E = 1.4426950408889634
VMEM = pl.BlockSpec(memory_space=pltpu.VMEM)
SMEM = pl.BlockSpec(memory_space=pltpu.SMEM)
HBM = pl.BlockSpec(memory_space=pltpu.HBM)
ANY = pl.BlockSpec(memory_space=pl.ANY)


def params(mib=24):
    return pltpu.CompilerParams(vmem_limit_bytes=mib << 20)


def absorb_kernel(nope_hbm, rope_hbm, w_hbm, out_ref, nope_ref, rope_ref, w_ref, sems):
    requests, heads, size = nope_ref.shape
    latent = w_ref.shape[2]
    rows = requests * heads
    step = 2 if heads % 2 == 0 else 1
    pieces = heads // step
    small = [
        pltpu.make_async_copy(nope_hbm, nope_ref, sems.at[pieces]),
        pltpu.make_async_copy(rope_hbm, rope_ref, sems.at[pieces + 1]),
    ]
    large = [
        pltpu.make_async_copy(
            w_hbm.at[pl.ds(i * step, step)], w_ref.at[pl.ds(i * step, step)], sems.at[i]
        )
        for i in range(pieces)
    ]
    for copy in small + large:
        copy.start()
    for copy in small:
        copy.wait()
    nope = nope_ref[...].astype(F32).reshape(rows, size)
    head = lax.broadcasted_iota(jnp.int32, (rows, size), 0) % heads
    out_ref[:, latent:] = rope_ref[...].astype(F32).reshape(rows, rope_ref.shape[2]).astype(BF16)
    total = jnp.zeros((rows, latent), F32)
    for i, copy in enumerate(large):
        wide = jnp.concatenate(
            [jnp.where(head == i * step + j, nope, 0.0) for j in range(step)], axis=1
        ).astype(BF16)
        copy.wait()
        weight = w_ref[i * step : (i + 1) * step].reshape(step * size, latent)
        total += jnp.dot(wide, weight, preferred_element_type=F32)
    out_ref[:, :latent] = total.astype(BF16)


def stage_kernel(
    cache_hbm, selected_hbm, lengths_hbm, after_ref,
    cache_ref, slots_ref, mask_ref, low_ref, high_ref, live_ref, selected_ref, lengths_ref, sems,
):
    requests, groups, picks = selected_ref.shape
    width, tokens = cache_ref.shape[1:]
    pages = tokens // PAGE
    rank = lax.axis_index("seq")
    copies = [
        pltpu.make_async_copy(selected_hbm, selected_ref, sems.at[0]),
        pltpu.make_async_copy(lengths_hbm, lengths_ref, sems.at[1]),
        *(
            pltpu.make_async_copy(cache_hbm.at[r], cache_ref.at[r], sems.at[2 + r])
            for r in range(requests)
        ),
    ]
    for copy in copies:
        copy.start()
    copies[0].wait()
    copies[1].wait()
    place = selected_ref[...].reshape(requests * groups, picks) - rank * pages
    here = (place >= 0) & (place < pages)
    bits = jnp.sum(
        jnp.where(here, jnp.left_shift(1, jnp.where(here, place, 0)), 0).astype(F32),
        axis=1,
        keepdims=True,
    ).astype(jnp.int32)
    lane = lax.broadcasted_iota(jnp.int32, (groups, tokens), 1)
    for r in range(requests):
        word = bits[r * groups : (r + 1) * groups]
        picked = jnp.bitwise_and(jnp.right_shift(word, lane // PAGE), 1) == 1
        live = lane + rank * tokens < lengths_ref[r]
        mask_ref[r * groups : (r + 1) * groups, :] = jnp.where(picked & live, 1.0, 0.0)
    first = (rank * pages + lax.broadcasted_iota(jnp.int32, (groups, pages), 1)) * PAGE
    row = lax.broadcasted_iota(jnp.int32, (tokens, width), 0) + rank * tokens
    for r in range(requests):
        live_ref[r] = jnp.where(first < lengths_ref[r], 1.0, 0.0)
        copies[2 + r].wait()
        slots = cache_ref[r].T
        slots_ref[r] = slots[:, : slots_ref.shape[2]]
        slots = slots.astype(F32)
        live = row < lengths_ref[r]
        slots = slots.reshape(pages, PAGE, width)
        slots = jnp.where(live.reshape(pages, PAGE, width), slots, slots[:, 0:1, :])
        low_ref[r] = jnp.min(slots, axis=1)
        high_ref[r] = jnp.max(slots, axis=1)


def split3(x):
    high = x.astype(BF16)
    rest = x - high.astype(F32)
    middle = rest.astype(BF16)
    return high, middle, (rest - middle.astype(F32)).astype(BF16)


def queries_of(blocks, request, heads):
    rows = slice(request * heads, (request + 1) * heads)
    return jnp.concatenate([b[rows] for b in blocks], axis=0)


def crossings(offset):
    return (1 if offset >> 1 else 0) + (offset & 1)


def group_of(offset, heads):
    source = jnp.bitwise_xor(lax.axis_index("seq"), offset)
    core = jnp.bitwise_xor(lax.axis_index("head"), crossings(offset) & 1)
    return (source * lax.axis_size("head") + core) * heads // GH


def attend_kernel(scale, heads, offsets, latent, *refs):
    count = len(offsets)
    block_refs = refs[:count]
    cache_ref, slots_ref, mask_ref, *out_refs = refs[count:]
    requests, _, tokens = cache_ref.shape
    groups = mask_ref.shape[0] // requests
    blocks = [b[...].astype(F32) for b in block_refs]
    scores = [
        jnp.dot(
            queries_of(blocks, r, heads).astype(BF16), cache_ref[r], preferred_element_type=F32
        )
        for r in range(requests)
    ]
    weights, shares, sums = [], [], []
    for r in range(requests):
        mask = jnp.concatenate(
            [
                jnp.broadcast_to(
                    mask_ref[pl.ds(r * groups + group_of(k, heads), 1), :], (heads, tokens)
                )
                for k in offsets
            ],
            axis=0,
        )
        masked = jnp.where(mask > 0.5, scores[r], NEG)
        top = jnp.max(masked, axis=1, keepdims=True)
        weight = jnp.exp2((masked - top) * (scale * LOG2E)).astype(BF16)
        total = jnp.sum(weight.astype(F32), axis=1, keepdims=True)
        weights.append(weight)
        shares.append(1.0 / total)
        sums.append(top * scale + jnp.log(total))
    outs = [
        jnp.dot(weights[r], slots_ref[r], preferred_element_type=F32) * shares[r]
        for r in range(requests)
    ]
    for i, k in enumerate(offsets):
        rows = slice(i * heads, (i + 1) * heads)
        out = jnp.concatenate([o[rows] for o in outs], axis=0)
        lse = jnp.concatenate([s[rows] for s in sums], axis=0)
        fill(out_refs[i], out, jnp.broadcast_to(lse, (lse.shape[0], LANES)))


def fill(ref, out, lse):
    latent = out.shape[1]
    ref[:, :latent] = out.astype(ref.dtype)
    ref[:, latent:] = packed(lse) if ref.dtype == BF16 else lse


def packed(lse):
    lane = lax.broadcasted_iota(jnp.int32, lse.shape, 1)
    high, middle, low = (p.astype(F32) for p in split3(lse))
    return jnp.where(lane == 0, high, jnp.where(lane == 1, middle, low)).astype(BF16)


def read(ref, latent):
    lse = ref[:, latent:].astype(F32)
    if ref.dtype == BF16:
        high, middle, low = (jnp.broadcast_to(lse[:, i : i + 1], lse.shape) for i in range(3))
        lse = high + middle + low
    return ref[:, :latent].astype(F32), lse


def merge(parts):
    top = functools.reduce(jnp.maximum, [s for _, s in parts])
    factors = [jnp.exp(s - top) for _, s in parts]
    total = functools.reduce(jnp.add, factors)
    share = 1.0 / total
    repeats = parts[0][0].shape[1] // LANES
    mixed = functools.reduce(
        jnp.add,
        [
            jnp.concatenate([factor * share] * repeats, axis=1) * out
            for factor, (out, _) in zip(factors, parts)
        ],
    )
    return mixed, top + jnp.log(total)


def pair_kernel(latent, got_ref, keep_ref, out_ref):
    fill(out_ref, *merge([read(got_ref, latent), read(keep_ref, latent)]))


def value_kernel(latent, heads, w_ref, *refs):
    part_refs, out_ref = refs[:-1], refs[-1]
    mixed = merge([read(ref, latent) for ref in part_refs])[0].astype(BF16)
    size = w_ref.shape[2]
    head = lax.broadcasted_iota(jnp.int32, (mixed.shape[0], size), 0) % heads
    weight = jnp.concatenate([w_ref[j] for j in range(heads)], axis=1)
    every = jnp.dot(mixed, weight, preferred_element_type=F32)
    out = every[:, :size]
    for j in range(1, heads):
        out = jnp.where(head == j, every[:, j * size : (j + 1) * size], out)
    out_ref[...] = out.reshape(out_ref.shape).astype(BF16)


def largest_kernel(mine_ref, other_ref, live_ref, bounds_ref):
    bounds_ref[...] = jnp.where(
        live_ref[...] > 0.5, jnp.maximum(mine_ref[...], other_ref[...]), 0.0
    )


def bounds_kernel(scale, heads, offsets, *refs):
    count = len(offsets)
    block_refs = refs[:count]
    low_ref, high_ref, after_ref, out_ref = refs[count:]
    requests, groups, pages = out_ref.shape
    blocks = [b[...].astype(F32) for b in block_refs]
    group = lax.broadcasted_iota(jnp.int32, (groups, pages), 0)
    dims = (((1,), (1,)), ((), ()))
    for r in range(requests):
        query = queries_of(blocks, r, heads)
        bound = lax.dot_general(
            jnp.maximum(query, 0.0).astype(BF16),
            high_ref[r].astype(BF16),
            dims,
            preferred_element_type=F32,
        ) + lax.dot_general(
            jnp.minimum(query, 0.0).astype(BF16),
            low_ref[r].astype(BF16),
            dims,
            preferred_element_type=F32,
        )
        bound = bound * scale
        best = jnp.full((groups, pages), NEG, F32)
        for i, k in enumerate(offsets):
            peak = jnp.max(bound[i * heads : (i + 1) * heads], axis=0, keepdims=True)
            best = jnp.where(group == group_of(k, heads), jnp.maximum(best, peak), best)
        out_ref[r] = best


def local(q_nope, q_rope, w_uk, w_uv, cache, lengths, selected):
    seq_count = lax.axis_size("seq")
    head_count = lax.axis_size("head")
    requests, heads, _ = q_nope.shape
    latent = w_uk.shape[2]
    width = cache.shape[2]
    tokens = cache.shape[1]
    pages = tokens // PAGE
    groups = selected.shape[1]
    rows = requests * heads
    scale = (q_nope.shape[2] + q_rope.shape[2]) ** (-0.5)
    assert seq_count & (seq_count - 1) == 0 and GH % heads == 0
    offsets = tuple(range(seq_count))
    far = tuple(reversed(range(2, seq_count, 2)))
    half = seq_count // 2
    slots = jnp.swapaxes(cache, 1, 2)

    q_nope, q_rope, w_uk, slots, lengths, selected = (
        pltpu.with_memory_space_constraint(x, pltpu.HBM)
        for x in (q_nope, q_rope, w_uk, slots, lengths, selected)
    )

    def swap(x, k, flip=1):
        pairs = [
            (i * head_count + c, (i ^ k) * head_count + (c ^ flip))
            for i in range(seq_count)
            for c in range(head_count)
        ]
        return lax.ppermute(x, ("seq", "head"), pairs)

    mine = pl.pallas_call(
        absorb_kernel,
        out_shape=jax.ShapeDtypeStruct((rows, width), BF16),
        in_specs=[HBM] * 3,
        out_specs=VMEM,
        scratch_shapes=[
            pltpu.VMEM(q_nope.shape, BF16),
            pltpu.VMEM(q_rope.shape, BF16),
            pltpu.VMEM(w_uk.shape, BF16),
            pltpu.SemaphoreType.DMA((heads + 2,)),
        ],
        compiler_params=params(),
        name="absorb",
    )(q_nope, q_rope, w_uk)
    block = {0: mine}
    for k in far:
        block[k] = swap(mine, k)
    near = far[-1]
    block[near + 1] = swap(mine, near + 1, 0)
    block[1] = swap(mine, 1)
    for k in far[:-1]:
        block[k + 1] = swap(block[k], 1)
    blocks = [block[k] for k in offsets]

    keys, values, mask, low, high, live = pl.pallas_call(
        stage_kernel,
        out_shape=(
            jax.ShapeDtypeStruct(slots.shape, BF16),
            jax.ShapeDtypeStruct((requests, tokens, latent), BF16),
            jax.ShapeDtypeStruct((requests * groups, tokens), F32),
            jax.ShapeDtypeStruct((requests, pages, width), F32),
            jax.ShapeDtypeStruct((requests, pages, width), F32),
            jax.ShapeDtypeStruct((requests, groups, pages), F32),
        ),
        in_specs=[HBM] * 3 + [ANY],
        out_specs=(VMEM,) * 6,
        scratch_shapes=[
            pltpu.VMEM(selected.shape, jnp.int32),
            pltpu.SMEM(lengths.shape, jnp.int32),
            pltpu.SemaphoreType.DMA((2 + requests,)),
        ],
        compiler_params=params(),
        name="stage_cache",
    )(slots, selected, lengths, block[near])

    parts = pl.pallas_call(
        functools.partial(attend_kernel, scale, heads, offsets, latent),
        out_shape=tuple(
            jax.ShapeDtypeStruct((rows, latent + LANES), BF16 if k % 2 else F32) for k in offsets
        ),
        in_specs=[VMEM] * (seq_count + 3),
        out_specs=(VMEM,) * seq_count,
        compiler_params=params(),
        name="attend",
    )(*blocks, keys, values, mask)

    got = {k: swap(parts[k + 1], 1) for k in far + (0,)}
    send = {
        k: pl.pallas_call(
            functools.partial(pair_kernel, latent),
            out_shape=jax.ShapeDtypeStruct((rows, latent + LANES), BF16),
            in_specs=[VMEM] * 2,
            out_specs=VMEM,
            compiler_params=params(),
            name="merge_pair",
        )(got[k], parts[k])
        for k in far
    }
    arrived = [swap(send[k], k) for k in far]

    bounds = pl.pallas_call(
        functools.partial(bounds_kernel, scale, heads, offsets),
        out_shape=jax.ShapeDtypeStruct((requests, groups, pages), F32),
        in_specs=[VMEM] * (seq_count + 2) + [ANY],
        out_specs=VMEM,
        compiler_params=params(),
        name="page_bounds",
    )(*blocks, low, high, send[far[-1]])
    others = lax.ppermute(bounds, "head", [(i, i ^ 1) for i in range(head_count)])
    largest = pl.pallas_call(
        largest_kernel,
        out_shape=jax.ShapeDtypeStruct((requests, groups, pages), F32),
        in_specs=[VMEM] * 3,
        out_specs=VMEM,
        compiler_params=params(),
        name="group_bounds",
    )(bounds, others, live)

    attended = pl.pallas_call(
        functools.partial(value_kernel, latent, heads),
        out_shape=jax.ShapeDtypeStruct((requests, heads, w_uv.shape[2]), BF16),
        in_specs=[VMEM] * (half + 2),
        out_specs=VMEM,
        compiler_params=params(),
        name="merge_and_value",
    )(w_uv, parts[0], got[0], *arrived)
    return attended, largest


def solution(mesh):
    assert mesh.shape["head"] == 2
    placed = (
        P("grp", ("seq", "head"), None),
        P("grp", ("seq", "head"), None),
        P(("seq", "head"), None, None),
        P(("seq", "head"), None, None),
        P("grp", "seq", None),
        P("grp"),
        P("grp", None, None),
    )
    return jax.shard_map(
        local,
        mesh=mesh,
        in_specs=placed,
        out_specs=(P("grp", ("seq", "head"), None), P("grp", None, "seq")),
        check_vma=False,
    )
```

```python
import functools

import jax
import jax.numpy as jnp
from jax import lax
from jax.experimental import pallas as pl
from jax.experimental.pallas import tpu as pltpu
from jax.sharding import PartitionSpec as P

GH = 16
PAGE = 64
NEG = -1e30
BF16 = jnp.bfloat16
F32 = jnp.float32
LANES = 128
LOG2E = 1.4426950408889634
VMEM = pl.BlockSpec(memory_space=pltpu.VMEM)
SMEM = pl.BlockSpec(memory_space=pltpu.SMEM)
HBM = pl.BlockSpec(memory_space=pltpu.HBM)
ANY = pl.BlockSpec(memory_space=pl.ANY)


def params(mib=24):
    return pltpu.CompilerParams(vmem_limit_bytes=mib << 20)


def absorb_kernel(nope_hbm, rope_hbm, w_hbm, out_ref, nope_ref, rope_ref, w_ref, sems):
    requests, heads, size = nope_ref.shape
    latent = w_ref.shape[2]
    rows = requests * heads
    step = 2 if heads % 2 == 0 else 1
    pieces = heads // step
    small = [
        pltpu.make_async_copy(nope_hbm, nope_ref, sems.at[pieces]),
        pltpu.make_async_copy(rope_hbm, rope_ref, sems.at[pieces + 1]),
    ]
    large = [
        pltpu.make_async_copy(
            w_hbm.at[pl.ds(i * step, step)], w_ref.at[pl.ds(i * step, step)], sems.at[i]
        )
        for i in range(pieces)
    ]
    for copy in small + large:
        copy.start()
    for copy in small:
        copy.wait()
    nope = nope_ref[...].astype(F32).reshape(rows, size)
    head = lax.broadcasted_iota(jnp.int32, (rows, size), 0) % heads
    out_ref[:, latent:] = rope_ref[...].astype(F32).reshape(rows, rope_ref.shape[2]).astype(BF16)
    total = jnp.zeros((rows, latent), F32)
    for i, copy in enumerate(large):
        wide = jnp.concatenate(
            [jnp.where(head == i * step + j, nope, 0.0) for j in range(step)], axis=1
        ).astype(BF16)
        copy.wait()
        weight = w_ref[i * step : (i + 1) * step].reshape(step * size, latent)
        total += jnp.dot(wide, weight, preferred_element_type=F32)
    out_ref[:, :latent] = total.astype(BF16)


def stage_kernel(
    cache_hbm, selected_hbm, lengths_hbm, after_ref,
    cache_ref, slots_ref, mask_ref, low_ref, high_ref, live_ref, selected_ref, lengths_ref, sems,
):
    requests, groups, picks = selected_ref.shape
    width, tokens = cache_ref.shape[1:]
    pages = tokens // PAGE
    rank = lax.axis_index("seq")
    copies = [
        pltpu.make_async_copy(selected_hbm, selected_ref, sems.at[0]),
        pltpu.make_async_copy(lengths_hbm, lengths_ref, sems.at[1]),
        *(
            pltpu.make_async_copy(cache_hbm.at[r], cache_ref.at[r], sems.at[2 + r])
            for r in range(requests)
        ),
    ]
    for copy in copies:
        copy.start()
    copies[0].wait()
    copies[1].wait()
    place = selected_ref[...].reshape(requests * groups, picks) - rank * pages
    here = (place >= 0) & (place < pages)
    bits = jnp.sum(
        jnp.where(here, jnp.left_shift(1, jnp.where(here, place, 0)), 0).astype(F32),
        axis=1,
        keepdims=True,
    ).astype(jnp.int32)
    lane = lax.broadcasted_iota(jnp.int32, (groups, tokens), 1)
    for r in range(requests):
        word = bits[r * groups : (r + 1) * groups]
        picked = jnp.bitwise_and(jnp.right_shift(word, lane // PAGE), 1) == 1
        live = lane + rank * tokens < lengths_ref[r]
        mask_ref[r * groups : (r + 1) * groups, :] = jnp.where(picked & live, 1.0, 0.0)
    first = (rank * pages + lax.broadcasted_iota(jnp.int32, (groups, pages), 1)) * PAGE
    row = lax.broadcasted_iota(jnp.int32, (tokens, width), 0) + rank * tokens
    for r in range(requests):
        live_ref[r] = jnp.where(first < lengths_ref[r], 1.0, 0.0)
        copies[2 + r].wait()
        slots = cache_ref[r].T
        slots_ref[r] = slots[:, : slots_ref.shape[2]]
        slots = slots.astype(F32)
        live = row < lengths_ref[r]
        slots = slots.reshape(pages, PAGE, width)
        slots = jnp.where(live.reshape(pages, PAGE, width), slots, slots[:, 0:1, :])
        low_ref[r] = jnp.min(slots, axis=1)
        high_ref[r] = jnp.max(slots, axis=1)


def split3(x):
    high = x.astype(BF16)
    rest = x - high.astype(F32)
    middle = rest.astype(BF16)
    return high, middle, (rest - middle.astype(F32)).astype(BF16)


def queries_of(blocks, request, heads):
    rows = slice(request * heads, (request + 1) * heads)
    return jnp.concatenate([b[rows] for b in blocks], axis=0)


def crossings(offset):
    return (1 if offset >> 1 else 0) + (offset & 1)


def group_of(offset, heads):
    source = jnp.bitwise_xor(lax.axis_index("seq"), offset)
    core = jnp.bitwise_xor(lax.axis_index("head"), crossings(offset) & 1)
    return (source * lax.axis_size("head") + core) * heads // GH


def attend_kernel(scale, heads, offsets, latent, *refs):
    count = len(offsets)
    block_refs = refs[:count]
    cache_ref, slots_ref, mask_ref, *out_refs = refs[count:]
    requests, _, tokens = cache_ref.shape
    groups = mask_ref.shape[0] // requests
    blocks = [b[...].astype(F32) for b in block_refs]
    scores = [
        jnp.dot(
            queries_of(blocks, r, heads).astype(BF16), cache_ref[r], preferred_element_type=F32
        )
        for r in range(requests)
    ]
    weights, shares, sums = [], [], []
    for r in range(requests):
        mask = jnp.concatenate(
            [
                jnp.broadcast_to(
                    mask_ref[pl.ds(r * groups + group_of(k, heads), 1), :], (heads, tokens)
                )
                for k in offsets
            ],
            axis=0,
        )
        masked = jnp.where(mask > 0.5, scores[r], NEG)
        top = jnp.max(masked, axis=1, keepdims=True)
        weight = jnp.exp2((masked - top) * (scale * LOG2E)).astype(BF16)
        total = jnp.sum(weight.astype(F32), axis=1, keepdims=True)
        weights.append(weight)
        shares.append(1.0 / total)
        sums.append(top * scale + jnp.log(total))
    outs = [
        jnp.dot(weights[r], slots_ref[r], preferred_element_type=F32) * shares[r]
        for r in range(requests)
    ]
    for i, k in enumerate(offsets):
        rows = slice(i * heads, (i + 1) * heads)
        out = jnp.concatenate([o[rows] for o in outs], axis=0)
        lse = jnp.concatenate([s[rows] for s in sums], axis=0)
        fill(out_refs[i], out, jnp.broadcast_to(lse, (lse.shape[0], LANES)))


def fill(ref, out, lse):
    latent = out.shape[1]
    ref[:, :latent] = out.astype(ref.dtype)
    ref[:, latent:] = packed(lse) if ref.dtype == BF16 else lse


def packed(lse):
    lane = lax.broadcasted_iota(jnp.int32, lse.shape, 1)
    high, middle, low = (p.astype(F32) for p in split3(lse))
    return jnp.where(lane == 0, high, jnp.where(lane == 1, middle, low)).astype(BF16)


def read(ref, latent):
    lse = ref[:, latent:].astype(F32)
    if ref.dtype == BF16:
        high, middle, low = (jnp.broadcast_to(lse[:, i : i + 1], lse.shape) for i in range(3))
        lse = high + middle + low
    return ref[:, :latent].astype(F32), lse


def merge(parts):
    top = functools.reduce(jnp.maximum, [s for _, s in parts])
    factors = [jnp.exp(s - top) for _, s in parts]
    total = functools.reduce(jnp.add, factors)
    share = 1.0 / total
    repeats = parts[0][0].shape[1] // LANES
    mixed = functools.reduce(
        jnp.add,
        [
            jnp.concatenate([factor * share] * repeats, axis=1) * out
            for factor, (out, _) in zip(factors, parts)
        ],
    )
    return mixed, top + jnp.log(total)


def pair_kernel(latent, got_ref, keep_ref, out_ref):
    fill(out_ref, *merge([read(got_ref, latent), read(keep_ref, latent)]))


def value_kernel(latent, heads, w_ref, *refs):
    part_refs, out_ref = refs[:-1], refs[-1]
    mixed = merge([read(ref, latent) for ref in part_refs])[0].astype(BF16)
    size = w_ref.shape[2]
    head = lax.broadcasted_iota(jnp.int32, (mixed.shape[0], size), 0) % heads
    weight = jnp.concatenate([w_ref[j] for j in range(heads)], axis=1)
    every = jnp.dot(mixed, weight, preferred_element_type=F32)
    out = every[:, :size]
    for j in range(1, heads):
        out = jnp.where(head == j, every[:, j * size : (j + 1) * size], out)
    out_ref[...] = out.reshape(out_ref.shape).astype(BF16)


def largest_kernel(mine_ref, other_ref, live_ref, bounds_ref):
    bounds_ref[...] = jnp.where(
        live_ref[...] > 0.5, jnp.maximum(mine_ref[...], other_ref[...]), 0.0
    )


def bounds_kernel(scale, heads, offsets, *refs):
    count = len(offsets)
    block_refs = refs[:count]
    low_ref, high_ref, after_ref, out_ref = refs[count:]
    requests, groups, pages = out_ref.shape
    blocks = [b[...].astype(F32) for b in block_refs]
    group = lax.broadcasted_iota(jnp.int32, (groups, pages), 0)
    dims = (((1,), (1,)), ((), ()))
    for r in range(requests):
        query = queries_of(blocks, r, heads)
        bound = lax.dot_general(
            jnp.maximum(query, 0.0).astype(BF16),
            high_ref[r].astype(BF16),
            dims,
            preferred_element_type=F32,
        ) + lax.dot_general(
            jnp.minimum(query, 0.0).astype(BF16),
            low_ref[r].astype(BF16),
            dims,
            preferred_element_type=F32,
        )
        bound = bound * scale
        best = jnp.full((groups, pages), NEG, F32)
        for i, k in enumerate(offsets):
            peak = jnp.max(bound[i * heads : (i + 1) * heads], axis=0, keepdims=True)
            best = jnp.where(group == group_of(k, heads), jnp.maximum(best, peak), best)
        out_ref[r] = best


def local(q_nope, q_rope, w_uk, w_uv, cache, lengths, selected):
    seq_count = lax.axis_size("seq")
    head_count = lax.axis_size("head")
    requests, heads, _ = q_nope.shape
    latent = w_uk.shape[2]
    width = cache.shape[2]
    tokens = cache.shape[1]
    pages = tokens // PAGE
    groups = selected.shape[1]
    rows = requests * heads
    scale = (q_nope.shape[2] + q_rope.shape[2]) ** (-0.5)
    assert seq_count & (seq_count - 1) == 0 and GH % heads == 0
    offsets = tuple(range(seq_count))
    far = tuple(reversed(range(2, seq_count, 2)))
    half = seq_count // 2
    slots = jnp.swapaxes(cache, 1, 2)

    q_nope, q_rope, w_uk, slots, lengths, selected = (
        pltpu.with_memory_space_constraint(x, pltpu.HBM)
        for x in (q_nope, q_rope, w_uk, slots, lengths, selected)
    )

    def swap(x, k, flip=1):
        pairs = [
            (i * head_count + c, (i ^ k) * head_count + (c ^ flip))
            for i in range(seq_count)
            for c in range(head_count)
        ]
        return lax.ppermute(x, ("seq", "head"), pairs)

    mine = pl.pallas_call(
        absorb_kernel,
        out_shape=jax.ShapeDtypeStruct((rows, width), BF16),
        in_specs=[HBM] * 3,
        out_specs=VMEM,
        scratch_shapes=[
            pltpu.VMEM(q_nope.shape, BF16),
            pltpu.VMEM(q_rope.shape, BF16),
            pltpu.VMEM(w_uk.shape, BF16),
            pltpu.SemaphoreType.DMA((heads + 2,)),
        ],
        compiler_params=params(),
        name="absorb",
    )(q_nope, q_rope, w_uk)
    block = {0: mine}
    for k in far:
        block[k] = swap(mine, k)
    near = far[-1]
    block[near + 1] = swap(mine, near + 1, 0)
    block[1] = swap(mine, 1)
    for k in far[:-1]:
        block[k + 1] = swap(block[k], 1)
    blocks = [block[k] for k in offsets]

    keys, values, mask, low, high, live = pl.pallas_call(
        stage_kernel,
        out_shape=(
            jax.ShapeDtypeStruct(slots.shape, BF16),
            jax.ShapeDtypeStruct((requests, tokens, latent), BF16),
            jax.ShapeDtypeStruct((requests * groups, tokens), F32),
            jax.ShapeDtypeStruct((requests, pages, width), F32),
            jax.ShapeDtypeStruct((requests, pages, width), F32),
            jax.ShapeDtypeStruct((requests, groups, pages), F32),
        ),
        in_specs=[HBM] * 3 + [ANY],
        out_specs=(VMEM,) * 6,
        scratch_shapes=[
            pltpu.VMEM(selected.shape, jnp.int32),
            pltpu.SMEM(lengths.shape, jnp.int32),
            pltpu.SemaphoreType.DMA((2 + requests,)),
        ],
        compiler_params=params(),
        name="stage_cache",
    )(slots, selected, lengths, block[near])

    parts = pl.pallas_call(
        functools.partial(attend_kernel, scale, heads, offsets, latent),
        out_shape=tuple(
            jax.ShapeDtypeStruct((rows, latent + LANES), BF16 if k % 2 else F32) for k in offsets
        ),
        in_specs=[VMEM] * (seq_count + 3),
        out_specs=(VMEM,) * seq_count,
        compiler_params=params(),
        name="attend",
    )(*blocks, keys, values, mask)

    got = {k: swap(parts[k + 1], 1) for k in far + (0,)}
    send = {
        k: pl.pallas_call(
            functools.partial(pair_kernel, latent),
            out_shape=jax.ShapeDtypeStruct((rows, latent + LANES), BF16),
            in_specs=[VMEM] * 2,
            out_specs=VMEM,
            compiler_params=params(),
            name="merge_pair",
        )(got[k], parts[k])
        for k in far
    }
    turns = far[:1] + far[:0:-1]
    arrived = [swap(send[k], k) for k in turns]

    bounds = pl.pallas_call(
        functools.partial(bounds_kernel, scale, heads, offsets),
        out_shape=jax.ShapeDtypeStruct((requests, groups, pages), F32),
        in_specs=[VMEM] * (seq_count + 2) + [ANY],
        out_specs=VMEM,
        compiler_params=params(),
        name="page_bounds",
    )(*blocks, low, high, send[far[-1]])
    others = lax.ppermute(bounds, "head", [(i, i ^ 1) for i in range(head_count)])
    largest = pl.pallas_call(
        largest_kernel,
        out_shape=jax.ShapeDtypeStruct((requests, groups, pages), F32),
        in_specs=[VMEM] * 3,
        out_specs=VMEM,
        compiler_params=params(),
        name="group_bounds",
    )(bounds, others, live)

    attended = pl.pallas_call(
        functools.partial(value_kernel, latent, heads),
        out_shape=jax.ShapeDtypeStruct((requests, heads, w_uv.shape[2]), BF16),
        in_specs=[VMEM] * (half + 2),
        out_specs=VMEM,
        compiler_params=params(),
        name="merge_and_value",
    )(w_uv, parts[0], got[0], *arrived)
    return attended, largest


def solution(mesh):
    assert mesh.shape["head"] == 2
    placed = (
        P("grp", ("seq", "head"), None),
        P("grp", ("seq", "head"), None),
        P(("seq", "head"), None, None),
        P(("seq", "head"), None, None),
        P("grp", "seq", None),
        P("grp"),
        P("grp", None, None),
    )
    return jax.shard_map(
        local,
        mesh=mesh,
        in_specs=placed,
        out_specs=(P("grp", ("seq", "head"), None), P("grp", None, "seq")),
        check_vma=False,
    )
```

```python
import functools

import jax
import jax.numpy as jnp
from jax import lax
from jax.experimental import pallas as pl
from jax.experimental.pallas import tpu as pltpu
from jax.sharding import PartitionSpec as P

GH = 16
PAGE = 64
NEG = -1e30
BF16 = jnp.bfloat16
F32 = jnp.float32
LANES = 128
LOG2E = 1.4426950408889634
VMEM = pl.BlockSpec(memory_space=pltpu.VMEM)
SMEM = pl.BlockSpec(memory_space=pltpu.SMEM)
HBM = pl.BlockSpec(memory_space=pltpu.HBM)
ANY = pl.BlockSpec(memory_space=pl.ANY)


def height(rows):
    return -(-rows // 16) * 16


def block_shape(rows, latent):
    return (latent // LANES * height(rows) + 16, LANES)


def put(ref, x, last):
    rows, width = x.shape
    for c in range(width // LANES):
        start = c * height(rows)
        ref[start : start + rows, :] = x[:, c * LANES : (c + 1) * LANES].astype(BF16)
    last = jnp.concatenate([last] * (16 // last.shape[0]), axis=0)
    ref[width // LANES * height(rows) :, :] = last.astype(BF16)


def take(ref, rows, width):
    x = ref[...].astype(F32)
    starts = [c * height(rows) for c in range(width // LANES)]
    return jnp.concatenate([x[a : a + rows] for a in starts], axis=1), x[-16:]


def params(mib=24):
    return pltpu.CompilerParams(vmem_limit_bytes=mib << 20)


def absorb_kernel(nope_hbm, rope_hbm, w_hbm, out_ref, nope_ref, rope_ref, w_ref, sems):
    requests, heads, size = nope_ref.shape
    latent = w_ref.shape[2]
    rows = requests * heads
    step = 2 if heads % 2 == 0 else 1
    pieces = heads // step
    small = [
        pltpu.make_async_copy(nope_hbm, nope_ref, sems.at[pieces]),
        pltpu.make_async_copy(rope_hbm, rope_ref, sems.at[pieces + 1]),
    ]
    large = [
        pltpu.make_async_copy(
            w_hbm.at[pl.ds(i * step, step)], w_ref.at[pl.ds(i * step, step)], sems.at[i]
        )
        for i in range(pieces)
    ]
    for copy in small + large:
        copy.start()
    for copy in small:
        copy.wait()
    nope = nope_ref[...].astype(F32).reshape(rows, size)
    head = lax.broadcasted_iota(jnp.int32, (rows, size), 0) % heads
    rope = rope_ref[...].astype(F32).reshape(rows, rope_ref.shape[2])
    fold = LANES // rope.shape[1]
    part = rows // fold
    rope = jnp.concatenate([rope[i * part : (i + 1) * part] for i in range(fold)], axis=1)
    total = jnp.zeros((rows, latent), F32)
    for i, copy in enumerate(large):
        wide = jnp.concatenate(
            [jnp.where(head == i * step + j, nope, 0.0) for j in range(step)], axis=1
        ).astype(BF16)
        copy.wait()
        weight = w_ref[i * step : (i + 1) * step].reshape(step * size, latent)
        total += jnp.dot(wide, weight, preferred_element_type=F32)
    put(out_ref, total, rope)


def stage_kernel(
    cache_hbm, selected_hbm, lengths_hbm, after_ref,
    cache_ref, slots_ref, mask_ref, low_ref, high_ref, live_ref, selected_ref, lengths_ref, sems,
):
    requests, groups, picks = selected_ref.shape
    width, tokens = cache_ref.shape[1:]
    pages = tokens // PAGE
    rank = lax.axis_index("seq")
    copies = [
        pltpu.make_async_copy(selected_hbm, selected_ref, sems.at[0]),
        pltpu.make_async_copy(lengths_hbm, lengths_ref, sems.at[1]),
        *(
            pltpu.make_async_copy(cache_hbm.at[r], cache_ref.at[r], sems.at[2 + r])
            for r in range(requests)
        ),
    ]
    for copy in copies:
        copy.start()
    copies[0].wait()
    copies[1].wait()
    place = selected_ref[...].reshape(requests * groups, picks) - rank * pages
    here = (place >= 0) & (place < pages)
    bits = jnp.sum(
        jnp.where(here, jnp.left_shift(1, jnp.where(here, place, 0)), 0).astype(F32),
        axis=1,
        keepdims=True,
    ).astype(jnp.int32)
    lane = lax.broadcasted_iota(jnp.int32, (groups, tokens), 1)
    for r in range(requests):
        word = bits[r * groups : (r + 1) * groups]
        picked = jnp.bitwise_and(jnp.right_shift(word, lane // PAGE), 1) == 1
        live = lane + rank * tokens < lengths_ref[r]
        mask_ref[r * groups : (r + 1) * groups, :] = jnp.where(picked & live, 1.0, 0.0)
    first = (rank * pages + lax.broadcasted_iota(jnp.int32, (groups, pages), 1)) * PAGE
    row = lax.broadcasted_iota(jnp.int32, (tokens, width), 0) + rank * tokens
    for r in range(requests):
        live_ref[r] = jnp.where(first < lengths_ref[r], 1.0, 0.0)
        copies[2 + r].wait()
        slots = cache_ref[r].T
        slots_ref[r] = slots[:, : slots_ref.shape[2]]
        slots = slots.astype(F32)
        live = row < lengths_ref[r]
        slots = slots.reshape(pages, PAGE, width)
        slots = jnp.where(live.reshape(pages, PAGE, width), slots, slots[:, 0:1, :])
        low_ref[r] = jnp.min(slots, axis=1)
        high_ref[r] = jnp.max(slots, axis=1)


def split3(x):
    high = x.astype(BF16)
    rest = x - high.astype(F32)
    middle = rest.astype(BF16)
    return high, middle, (rest - middle.astype(F32)).astype(BF16)


def queries_of(blocks, request, heads, width):
    found = []
    for latent, rope in blocks:
        size = width - latent.shape[1]
        part = latent.shape[0] * size // LANES
        column, row = divmod(request * heads, part)
        found.append(
            jnp.concatenate(
                [
                    latent[request * heads : (request + 1) * heads],
                    rope[row : row + heads, column * size : (column + 1) * size],
                ],
                axis=1,
            )
        )
    return jnp.concatenate(found, axis=0)


def crossings(offset):
    return (1 if offset >> 1 else 0) + (offset & 1)


def group_of(offset, heads):
    source = jnp.bitwise_xor(lax.axis_index("seq"), offset)
    core = jnp.bitwise_xor(lax.axis_index("head"), crossings(offset) & 1)
    return (source * lax.axis_size("head") + core) * heads // GH


def attend_kernel(scale, heads, offsets, latent, *refs):
    count = len(offsets)
    block_refs = refs[:count]
    cache_ref, slots_ref, mask_ref, *out_refs = refs[count:]
    requests, width, tokens = cache_ref.shape
    groups = mask_ref.shape[0] // requests
    blocks = [take(b, requests * heads, latent) for b in block_refs]
    scores = [
        jnp.dot(
            queries_of(blocks, r, heads, width).astype(BF16),
            cache_ref[r],
            preferred_element_type=F32,
        )
        for r in range(requests)
    ]
    weights, shares, sums = [], [], []
    for r in range(requests):
        mask = jnp.concatenate(
            [
                jnp.broadcast_to(
                    mask_ref[pl.ds(r * groups + group_of(k, heads), 1), :], (heads, tokens)
                )
                for k in offsets
            ],
            axis=0,
        )
        masked = jnp.where(mask > 0.5, scores[r], NEG)
        top = jnp.max(masked, axis=1, keepdims=True)
        weight = jnp.exp2((masked - top) * (scale * LOG2E)).astype(BF16)
        total = jnp.sum(weight.astype(F32), axis=1, keepdims=True)
        weights.append(weight)
        shares.append(1.0 / total)
        sums.append(top * scale + jnp.log(total))
    outs = [
        jnp.dot(weights[r], slots_ref[r], preferred_element_type=F32) * shares[r]
        for r in range(requests)
    ]
    for i, k in enumerate(offsets):
        rows = slice(i * heads, (i + 1) * heads)
        out = jnp.concatenate([o[rows] for o in outs], axis=0)
        lse = jnp.concatenate([s[rows] for s in sums], axis=0)
        fill(out_refs[i], out, jnp.broadcast_to(lse, (lse.shape[0], LANES)))


def fill(ref, out, lse):
    if ref.dtype == BF16:
        put(ref, out, packed(lse))
    else:
        ref[:, : out.shape[1]] = out
        ref[:, out.shape[1] :] = lse


def packed(lse):
    count = lse.shape[0] // 8
    span = LANES // count
    lane = lax.broadcasted_iota(jnp.int32, (8, LANES), 1)
    value = lse[:8]
    for i in range(1, count):
        value = jnp.where(lane // span == i, lse[i * 8 : (i + 1) * 8], value)
    high, middle, low = (p.astype(F32) for p in split3(value))
    place = lane % span
    return jnp.where(place == 0, high, jnp.where(place == 1, middle, low))


def unpacked(last, rows):
    count = rows // 8
    span = LANES // count
    found = []
    for i in range(count):
        high, middle, low = (
            jnp.broadcast_to(last[:8, i * span + j : i * span + j + 1], (8, LANES))
            for j in range(3)
        )
        found.append(high + middle + low)
    return jnp.concatenate(found, axis=0)


def read(ref, rows, latent):
    if ref.dtype == BF16:
        out, last = take(ref, rows, latent)
        return out, unpacked(last, rows)
    return ref[:, :latent], ref[:, latent:]


def merge(parts):
    top = functools.reduce(jnp.maximum, [s for _, s in parts])
    factors = [jnp.exp(s - top) for _, s in parts]
    total = functools.reduce(jnp.add, factors)
    share = 1.0 / total
    repeats = parts[0][0].shape[1] // LANES
    mixed = functools.reduce(
        jnp.add,
        [
            jnp.concatenate([factor * share] * repeats, axis=1) * out
            for factor, (out, _) in zip(factors, parts)
        ],
    )
    return mixed, top + jnp.log(total)


def pair_kernel(rows, latent, got_ref, keep_ref, out_ref):
    fill(out_ref, *merge([read(got_ref, rows, latent), read(keep_ref, rows, latent)]))


def value_kernel(rows, latent, heads, w_ref, *refs):
    part_refs, out_ref = refs[:-1], refs[-1]
    mixed = merge([read(ref, rows, latent) for ref in part_refs])[0].astype(BF16)
    size = w_ref.shape[2]
    head = lax.broadcasted_iota(jnp.int32, (mixed.shape[0], size), 0) % heads
    weight = jnp.concatenate([w_ref[j] for j in range(heads)], axis=1)
    every = jnp.dot(mixed, weight, preferred_element_type=F32)
    out = every[:, :size]
    for j in range(1, heads):
        out = jnp.where(head == j, every[:, j * size : (j + 1) * size], out)
    out_ref[...] = out.reshape(out_ref.shape).astype(BF16)


def largest_kernel(mine_ref, other_ref, live_ref, bounds_ref):
    bounds_ref[...] = jnp.where(
        live_ref[...] > 0.5, jnp.maximum(mine_ref[...], other_ref[...]), 0.0
    )


def bounds_kernel(scale, heads, offsets, latent, *refs):
    count = len(offsets)
    block_refs = refs[:count]
    low_ref, high_ref, after_ref, out_ref = refs[count:]
    requests, groups, pages = out_ref.shape
    width = low_ref.shape[2]
    blocks = [take(b, requests * heads, latent) for b in block_refs]
    group = lax.broadcasted_iota(jnp.int32, (groups, pages), 0)
    dims = (((1,), (1,)), ((), ()))
    for r in range(requests):
        query = queries_of(blocks, r, heads, width)
        bound = lax.dot_general(
            jnp.maximum(query, 0.0).astype(BF16),
            high_ref[r].astype(BF16),
            dims,
            preferred_element_type=F32,
        ) + lax.dot_general(
            jnp.minimum(query, 0.0).astype(BF16),
            low_ref[r].astype(BF16),
            dims,
            preferred_element_type=F32,
        )
        bound = bound * scale
        best = jnp.full((groups, pages), NEG, F32)
        for i, k in enumerate(offsets):
            peak = jnp.max(bound[i * heads : (i + 1) * heads], axis=0, keepdims=True)
            best = jnp.where(group == group_of(k, heads), jnp.maximum(best, peak), best)
        out_ref[r] = best


def local(q_nope, q_rope, w_uk, w_uv, cache, lengths, selected):
    seq_count = lax.axis_size("seq")
    head_count = lax.axis_size("head")
    requests, heads, _ = q_nope.shape
    latent = w_uk.shape[2]
    tokens = cache.shape[1]
    pages = tokens // PAGE
    groups = selected.shape[1]
    rows = requests * heads
    scale = (q_nope.shape[2] + q_rope.shape[2]) ** (-0.5)
    assert seq_count & (seq_count - 1) == 0 and GH % heads == 0
    offsets = tuple(range(seq_count))
    far = tuple(reversed(range(2, seq_count, 2)))
    half = seq_count // 2
    slots = jnp.swapaxes(cache, 1, 2)

    q_nope, q_rope, w_uk, slots, lengths, selected = (
        pltpu.with_memory_space_constraint(x, pltpu.HBM)
        for x in (q_nope, q_rope, w_uk, slots, lengths, selected)
    )

    def swap(x, k, flip=1):
        pairs = [
            (i * head_count + c, (i ^ k) * head_count + (c ^ flip))
            for i in range(seq_count)
            for c in range(head_count)
        ]
        return lax.ppermute(x, ("seq", "head"), pairs)

    mine = pl.pallas_call(
        absorb_kernel,
        out_shape=jax.ShapeDtypeStruct(block_shape(rows, latent), BF16),
        in_specs=[HBM] * 3,
        out_specs=VMEM,
        scratch_shapes=[
            pltpu.VMEM(q_nope.shape, BF16),
            pltpu.VMEM(q_rope.shape, BF16),
            pltpu.VMEM(w_uk.shape, BF16),
            pltpu.SemaphoreType.DMA((heads + 2,)),
        ],
        compiler_params=params(),
        name="absorb",
    )(q_nope, q_rope, w_uk)
    block = {0: mine}
    for k in far:
        block[k] = swap(mine, k)
    near = far[-1]
    block[near + 1] = swap(mine, near + 1, 0)
    block[1] = swap(mine, 1)
    for k in far[:-1]:
        block[k + 1] = swap(block[k], 1)
    blocks = [block[k] for k in offsets]

    keys, values, mask, low, high, live = pl.pallas_call(
        stage_kernel,
        out_shape=(
            jax.ShapeDtypeStruct(slots.shape, BF16),
            jax.ShapeDtypeStruct((requests, tokens, latent), BF16),
            jax.ShapeDtypeStruct((requests * groups, tokens), F32),
            jax.ShapeDtypeStruct((requests, pages, cache.shape[2]), F32),
            jax.ShapeDtypeStruct((requests, pages, cache.shape[2]), F32),
            jax.ShapeDtypeStruct((requests, groups, pages), F32),
        ),
        in_specs=[HBM] * 3 + [ANY],
        out_specs=(VMEM,) * 6,
        scratch_shapes=[
            pltpu.VMEM(selected.shape, jnp.int32),
            pltpu.SMEM(lengths.shape, jnp.int32),
            pltpu.SemaphoreType.DMA((2 + requests,)),
        ],
        compiler_params=params(),
        name="stage_cache",
    )(slots, selected, lengths, block[near])

    parts = pl.pallas_call(
        functools.partial(attend_kernel, scale, heads, offsets, latent),
        out_shape=tuple(
            jax.ShapeDtypeStruct(block_shape(rows, latent), BF16)
            if k % 2
            else jax.ShapeDtypeStruct((rows, latent + LANES), F32)
            for k in offsets
        ),
        in_specs=[VMEM] * (seq_count + 3),
        out_specs=(VMEM,) * seq_count,
        compiler_params=params(),
        name="attend",
    )(*blocks, keys, values, mask)

    got = {k: swap(parts[k + 1], 1) for k in far + (0,)}
    send = {
        k: pl.pallas_call(
            functools.partial(pair_kernel, rows, latent),
            out_shape=jax.ShapeDtypeStruct(block_shape(rows, latent), BF16),
            in_specs=[VMEM] * 2,
            out_specs=VMEM,
            compiler_params=params(),
            name="merge_pair",
        )(got[k], parts[k])
        for k in far
    }
    turns = far[:1] + far[:0:-1]
    arrived = [swap(send[k], k) for k in turns]

    bounds = pl.pallas_call(
        functools.partial(bounds_kernel, scale, heads, offsets, latent),
        out_shape=jax.ShapeDtypeStruct((requests, groups, pages), F32),
        in_specs=[VMEM] * (seq_count + 2) + [ANY],
        out_specs=VMEM,
        compiler_params=params(),
        name="page_bounds",
    )(*blocks, low, high, send[far[-1]])
    others = lax.ppermute(bounds, "head", [(i, i ^ 1) for i in range(head_count)])
    largest = pl.pallas_call(
        largest_kernel,
        out_shape=jax.ShapeDtypeStruct((requests, groups, pages), F32),
        in_specs=[VMEM] * 3,
        out_specs=VMEM,
        compiler_params=params(),
        name="group_bounds",
    )(bounds, others, live)

    attended = pl.pallas_call(
        functools.partial(value_kernel, rows, latent, heads),
        out_shape=jax.ShapeDtypeStruct((requests, heads, w_uv.shape[2]), BF16),
        in_specs=[VMEM] * (half + 2),
        out_specs=VMEM,
        compiler_params=params(),
        name="merge_and_value",
    )(w_uv, parts[0], got[0], *arrived)
    return attended, largest


def solution(mesh):
    assert mesh.shape["head"] == 2
    placed = (
        P("grp", ("seq", "head"), None),
        P("grp", ("seq", "head"), None),
        P(("seq", "head"), None, None),
        P(("seq", "head"), None, None),
        P("grp", "seq", None),
        P("grp"),
        P("grp", None, None),
    )
    return jax.shard_map(
        local,
        mesh=mesh,
        in_specs=placed,
        out_specs=(P("grp", ("seq", "head"), None), P("grp", None, "seq")),
        check_vma=False,
    )
```

```python
import functools

import jax
import jax.numpy as jnp
from jax import lax
from jax.experimental import pallas as pl
from jax.experimental.pallas import tpu as pltpu
from jax.sharding import PartitionSpec as P

GH = 16
PAGE = 64
NEG = -1e30
BF16 = jnp.bfloat16
F32 = jnp.float32
LANES = 128
LOG2E = 1.4426950408889634
VMEM = pl.BlockSpec(memory_space=pltpu.VMEM)
SMEM = pl.BlockSpec(memory_space=pltpu.SMEM)
HBM = pl.BlockSpec(memory_space=pltpu.HBM)
ANY = pl.BlockSpec(memory_space=pl.ANY)


def height(rows):
    return -(-rows // 16) * 16


def block_shape(rows, latent):
    return (latent // LANES * height(rows) + 16, LANES)


def put(ref, x, last):
    rows, width = x.shape
    for c in range(width // LANES):
        start = c * height(rows)
        ref[start : start + rows, :] = x[:, c * LANES : (c + 1) * LANES].astype(BF16)
    last = jnp.concatenate([last] * (16 // last.shape[0]), axis=0)
    ref[width // LANES * height(rows) :, :] = last.astype(BF16)


def take(ref, rows, width):
    x = ref[...].astype(F32)
    starts = [c * height(rows) for c in range(width // LANES)]
    return jnp.concatenate([x[a : a + rows] for a in starts], axis=1), x[-16:]


def params(mib=24):
    return pltpu.CompilerParams(vmem_limit_bytes=mib << 20)


def absorb_kernel(nope_hbm, rope_hbm, w_hbm, out_ref, nope_ref, rope_ref, w_ref, sems):
    requests, heads, size = nope_ref.shape
    latent = w_ref.shape[2]
    rows = requests * heads
    step = 2 if heads % 2 == 0 else 1
    pieces = heads // step
    small = [
        pltpu.make_async_copy(nope_hbm, nope_ref, sems.at[pieces]),
        pltpu.make_async_copy(rope_hbm, rope_ref, sems.at[pieces + 1]),
    ]
    large = [
        pltpu.make_async_copy(
            w_hbm.at[pl.ds(i * step, step)], w_ref.at[pl.ds(i * step, step)], sems.at[i]
        )
        for i in range(pieces)
    ]
    for copy in large + small:
        copy.start()
    for copy in small:
        copy.wait()
    nope = nope_ref[...].astype(F32).reshape(rows, size)
    head = lax.broadcasted_iota(jnp.int32, (rows, size), 0) % heads
    rope = rope_ref[...].astype(F32).reshape(rows, rope_ref.shape[2])
    fold = LANES // rope.shape[1]
    part = rows // fold
    rope = jnp.concatenate([rope[i * part : (i + 1) * part] for i in range(fold)], axis=1)
    wides = [
        jnp.concatenate(
            [jnp.where(head == i * step + j, nope, 0.0) for j in range(step)], axis=1
        ).astype(BF16)
        for i in range(pieces)
    ]
    total = jnp.zeros((rows, latent), F32)
    for i, copy in enumerate(large):
        copy.wait()
        weight = w_ref[i * step : (i + 1) * step].reshape(step * size, latent)
        total += jnp.dot(wides[i], weight, preferred_element_type=F32)
    put(out_ref, total, rope)


def stage_kernel(
    cache_hbm, selected_hbm, lengths_hbm, after_ref,
    cache_ref, slots_ref, mask_ref, low_ref, high_ref, live_ref, selected_ref, lengths_ref, sems,
):
    requests, groups, picks = selected_ref.shape
    width, tokens = cache_ref.shape[1:]
    pages = tokens // PAGE
    rank = lax.axis_index("seq")
    copies = [
        pltpu.make_async_copy(selected_hbm, selected_ref, sems.at[0]),
        pltpu.make_async_copy(lengths_hbm, lengths_ref, sems.at[1]),
        *(
            pltpu.make_async_copy(cache_hbm.at[r], cache_ref.at[r], sems.at[2 + r])
            for r in range(requests)
        ),
    ]
    for copy in copies:
        copy.start()
    copies[0].wait()
    copies[1].wait()
    place = selected_ref[...].reshape(requests * groups, picks) - rank * pages
    here = (place >= 0) & (place < pages)
    bits = jnp.sum(
        jnp.where(here, jnp.left_shift(1, jnp.where(here, place, 0)), 0).astype(F32),
        axis=1,
        keepdims=True,
    ).astype(jnp.int32)
    lane = lax.broadcasted_iota(jnp.int32, (groups, tokens), 1)
    for r in range(requests):
        word = bits[r * groups : (r + 1) * groups]
        picked = jnp.bitwise_and(jnp.right_shift(word, lane // PAGE), 1) == 1
        live = lane + rank * tokens < lengths_ref[r]
        mask_ref[r * groups : (r + 1) * groups, :] = jnp.where(picked & live, 1.0, 0.0)
    first = (rank * pages + lax.broadcasted_iota(jnp.int32, (groups, pages), 1)) * PAGE
    row = lax.broadcasted_iota(jnp.int32, (tokens, width), 0) + rank * tokens
    for r in range(requests):
        live_ref[r] = jnp.where(first < lengths_ref[r], 1.0, 0.0)
        copies[2 + r].wait()
        slots = cache_ref[r].T
        slots_ref[r] = slots[:, : slots_ref.shape[2]]
        slots = slots.astype(F32)
        live = row < lengths_ref[r]
        slots = slots.reshape(pages, PAGE, width)
        slots = jnp.where(live.reshape(pages, PAGE, width), slots, slots[:, 0:1, :])
        low_ref[r] = jnp.min(slots, axis=1)
        high_ref[r] = jnp.max(slots, axis=1)


def split3(x):
    high = x.astype(BF16)
    rest = x - high.astype(F32)
    middle = rest.astype(BF16)
    return high, middle, (rest - middle.astype(F32)).astype(BF16)


def queries_of(blocks, request, heads, width):
    found = []
    for latent, rope in blocks:
        size = width - latent.shape[1]
        part = latent.shape[0] * size // LANES
        column, row = divmod(request * heads, part)
        found.append(
            jnp.concatenate(
                [
                    latent[request * heads : (request + 1) * heads],
                    rope[row : row + heads, column * size : (column + 1) * size],
                ],
                axis=1,
            )
        )
    return jnp.concatenate(found, axis=0)


def crossings(offset):
    return (1 if offset >> 1 else 0) + (offset & 1)


def group_of(offset, heads):
    source = jnp.bitwise_xor(lax.axis_index("seq"), offset)
    core = jnp.bitwise_xor(lax.axis_index("head"), crossings(offset) & 1)
    return (source * lax.axis_size("head") + core) * heads // GH


def attend_kernel(scale, heads, offsets, latent, *refs):
    count = len(offsets)
    block_refs = refs[:count]
    cache_ref, slots_ref, mask_ref, *out_refs = refs[count:]
    requests, width, tokens = cache_ref.shape
    groups = mask_ref.shape[0] // requests
    blocks = [take(b, requests * heads, latent) for b in block_refs]
    scores = [
        jnp.dot(
            queries_of(blocks, r, heads, width).astype(BF16),
            cache_ref[r],
            preferred_element_type=F32,
        )
        for r in range(requests)
    ]
    weights, shares, sums = [], [], []
    for r in range(requests):
        mask = jnp.concatenate(
            [
                jnp.broadcast_to(
                    mask_ref[pl.ds(r * groups + group_of(k, heads), 1), :], (heads, tokens)
                )
                for k in offsets
            ],
            axis=0,
        )
        masked = jnp.where(mask > 0.5, scores[r], NEG)
        top = jnp.max(masked, axis=1, keepdims=True)
        weight = jnp.exp2((masked - top) * (scale * LOG2E)).astype(BF16)
        total = jnp.sum(weight.astype(F32), axis=1, keepdims=True)
        weights.append(weight)
        shares.append(1.0 / total)
        sums.append(top * scale + jnp.log(total))
    outs = [
        jnp.dot(weights[r], slots_ref[r], preferred_element_type=F32) * shares[r]
        for r in range(requests)
    ]
    for i, k in enumerate(offsets):
        rows = slice(i * heads, (i + 1) * heads)
        out = jnp.concatenate([o[rows] for o in outs], axis=0)
        lse = jnp.concatenate([s[rows] for s in sums], axis=0)
        fill(out_refs[i], out, jnp.broadcast_to(lse, (lse.shape[0], LANES)))


def fill(ref, out, lse):
    if ref.dtype == BF16:
        put(ref, out, packed(lse))
    else:
        ref[:, : out.shape[1]] = out
        ref[:, out.shape[1] :] = lse


def packed(lse):
    count = lse.shape[0] // 8
    span = LANES // count
    lane = lax.broadcasted_iota(jnp.int32, (8, LANES), 1)
    value = lse[:8]
    for i in range(1, count):
        value = jnp.where(lane // span == i, lse[i * 8 : (i + 1) * 8], value)
    high, middle, low = (p.astype(F32) for p in split3(value))
    place = lane % span
    return jnp.where(place == 0, high, jnp.where(place == 1, middle, low))


def unpacked(last, rows):
    count = rows // 8
    span = LANES // count
    found = []
    for i in range(count):
        high, middle, low = (
            jnp.broadcast_to(last[:8, i * span + j : i * span + j + 1], (8, LANES))
            for j in range(3)
        )
        found.append(high + middle + low)
    return jnp.concatenate(found, axis=0)


def read(ref, rows, latent):
    if ref.dtype == BF16:
        out, last = take(ref, rows, latent)
        return out, unpacked(last, rows)
    return ref[:, :latent], ref[:, latent:]


def merge(parts):
    top = functools.reduce(jnp.maximum, [s for _, s in parts])
    factors = [jnp.exp(s - top) for _, s in parts]
    total = functools.reduce(jnp.add, factors)
    share = 1.0 / total
    repeats = parts[0][0].shape[1] // LANES
    mixed = functools.reduce(
        jnp.add,
        [
            jnp.concatenate([factor * share] * repeats, axis=1) * out
            for factor, (out, _) in zip(factors, parts)
        ],
    )
    return mixed, top + jnp.log(total)


def pair_kernel(rows, latent, got_ref, keep_ref, out_ref):
    fill(out_ref, *merge([read(got_ref, rows, latent), read(keep_ref, rows, latent)]))


def value_kernel(rows, latent, heads, w_ref, *refs):
    part_refs, out_ref = refs[:-1], refs[-1]
    mixed = merge([read(ref, rows, latent) for ref in part_refs])[0].astype(BF16)
    size = w_ref.shape[2]
    head = lax.broadcasted_iota(jnp.int32, (mixed.shape[0], size), 0) % heads
    weight = jnp.concatenate([w_ref[j] for j in range(heads)], axis=1)
    every = jnp.dot(mixed, weight, preferred_element_type=F32)
    out = every[:, :size]
    for j in range(1, heads):
        out = jnp.where(head == j, every[:, j * size : (j + 1) * size], out)
    out_ref[...] = out.reshape(out_ref.shape).astype(BF16)


def largest_kernel(mine_ref, other_ref, live_ref, bounds_ref):
    bounds_ref[...] = jnp.where(
        live_ref[...] > 0.5, jnp.maximum(mine_ref[...], other_ref[...]), 0.0
    )


def bounds_kernel(scale, heads, offsets, latent, *refs):
    count = len(offsets)
    block_refs = refs[:count]
    low_ref, high_ref, after_ref, out_ref = refs[count:]
    requests, groups, pages = out_ref.shape
    width = low_ref.shape[2]
    blocks = [take(b, requests * heads, latent) for b in block_refs]
    group = lax.broadcasted_iota(jnp.int32, (groups, pages), 0)
    dims = (((1,), (1,)), ((), ()))
    for r in range(requests):
        query = queries_of(blocks, r, heads, width)
        bound = lax.dot_general(
            jnp.maximum(query, 0.0).astype(BF16),
            high_ref[r].astype(BF16),
            dims,
            preferred_element_type=F32,
        ) + lax.dot_general(
            jnp.minimum(query, 0.0).astype(BF16),
            low_ref[r].astype(BF16),
            dims,
            preferred_element_type=F32,
        )
        bound = bound * scale
        best = jnp.full((groups, pages), NEG, F32)
        for i, k in enumerate(offsets):
            peak = jnp.max(bound[i * heads : (i + 1) * heads], axis=0, keepdims=True)
            best = jnp.where(group == group_of(k, heads), jnp.maximum(best, peak), best)
        out_ref[r] = best


def local(q_nope, q_rope, w_uk, w_uv, cache, lengths, selected):
    seq_count = lax.axis_size("seq")
    head_count = lax.axis_size("head")
    requests, heads, _ = q_nope.shape
    latent = w_uk.shape[2]
    tokens = cache.shape[1]
    pages = tokens // PAGE
    groups = selected.shape[1]
    rows = requests * heads
    scale = (q_nope.shape[2] + q_rope.shape[2]) ** (-0.5)
    assert seq_count & (seq_count - 1) == 0 and GH % heads == 0
    offsets = tuple(range(seq_count))
    far = tuple(reversed(range(2, seq_count, 2)))
    half = seq_count // 2
    slots = jnp.swapaxes(cache, 1, 2)

    q_nope, q_rope, w_uk, slots, lengths, selected = (
        pltpu.with_memory_space_constraint(x, pltpu.HBM)
        for x in (q_nope, q_rope, w_uk, slots, lengths, selected)
    )

    def swap(x, k, flip=1):
        pairs = [
            (i * head_count + c, (i ^ k) * head_count + (c ^ flip))
            for i in range(seq_count)
            for c in range(head_count)
        ]
        return lax.ppermute(x, ("seq", "head"), pairs)

    mine = pl.pallas_call(
        absorb_kernel,
        out_shape=jax.ShapeDtypeStruct(block_shape(rows, latent), BF16),
        in_specs=[HBM] * 3,
        out_specs=VMEM,
        scratch_shapes=[
            pltpu.VMEM(q_nope.shape, BF16),
            pltpu.VMEM(q_rope.shape, BF16),
            pltpu.VMEM(w_uk.shape, BF16),
            pltpu.SemaphoreType.DMA((heads + 2,)),
        ],
        compiler_params=params(),
        name="absorb",
    )(q_nope, q_rope, w_uk)
    block = {0: mine}
    for k in far:
        block[k] = swap(mine, k)
    near = far[-1]
    block[near + 1] = swap(mine, near + 1, 0)
    block[1] = swap(mine, 1)
    for k in far[:-1]:
        block[k + 1] = swap(block[k], 1)
    blocks = [block[k] for k in offsets]

    keys, values, mask, low, high, live = pl.pallas_call(
        stage_kernel,
        out_shape=(
            jax.ShapeDtypeStruct(slots.shape, BF16),
            jax.ShapeDtypeStruct((requests, tokens, latent), BF16),
            jax.ShapeDtypeStruct((requests * groups, tokens), F32),
            jax.ShapeDtypeStruct((requests, pages, cache.shape[2]), F32),
            jax.ShapeDtypeStruct((requests, pages, cache.shape[2]), F32),
            jax.ShapeDtypeStruct((requests, groups, pages), F32),
        ),
        in_specs=[HBM] * 3 + [ANY],
        out_specs=(VMEM,) * 6,
        scratch_shapes=[
            pltpu.VMEM(selected.shape, jnp.int32),
            pltpu.SMEM(lengths.shape, jnp.int32),
            pltpu.SemaphoreType.DMA((2 + requests,)),
        ],
        compiler_params=params(),
        name="stage_cache",
    )(slots, selected, lengths, block[near])

    parts = pl.pallas_call(
        functools.partial(attend_kernel, scale, heads, offsets, latent),
        out_shape=tuple(
            jax.ShapeDtypeStruct(block_shape(rows, latent), BF16)
            if k % 2
            else jax.ShapeDtypeStruct((rows, latent + LANES), F32)
            for k in offsets
        ),
        in_specs=[VMEM] * (seq_count + 3),
        out_specs=(VMEM,) * seq_count,
        compiler_params=params(),
        name="attend",
    )(*blocks, keys, values, mask)

    got = {k: swap(parts[k + 1], 1) for k in far + (0,)}
    send = {
        k: pl.pallas_call(
            functools.partial(pair_kernel, rows, latent),
            out_shape=jax.ShapeDtypeStruct(block_shape(rows, latent), BF16),
            in_specs=[VMEM] * 2,
            out_specs=VMEM,
            compiler_params=params(),
            name="merge_pair",
        )(got[k], parts[k])
        for k in far
    }
    turns = far[:1] + far[:0:-1]
    arrived = [swap(send[k], k) for k in turns]

    bounds = pl.pallas_call(
        functools.partial(bounds_kernel, scale, heads, offsets, latent),
        out_shape=jax.ShapeDtypeStruct((requests, groups, pages), F32),
        in_specs=[VMEM] * (seq_count + 2) + [ANY],
        out_specs=VMEM,
        compiler_params=params(),
        name="page_bounds",
    )(*blocks, low, high, send[far[-1]])
    others = lax.ppermute(bounds, "head", [(i, i ^ 1) for i in range(head_count)])
    largest = pl.pallas_call(
        largest_kernel,
        out_shape=jax.ShapeDtypeStruct((requests, groups, pages), F32),
        in_specs=[VMEM] * 3,
        out_specs=VMEM,
        compiler_params=params(),
        name="group_bounds",
    )(bounds, others, live)

    attended = pl.pallas_call(
        functools.partial(value_kernel, rows, latent, heads),
        out_shape=jax.ShapeDtypeStruct((requests, heads, w_uv.shape[2]), BF16),
        in_specs=[VMEM] * (half + 2),
        out_specs=VMEM,
        compiler_params=params(),
        name="merge_and_value",
    )(w_uv, parts[0], got[0], *arrived)
    return attended, largest


def solution(mesh):
    assert mesh.shape["head"] == 2
    placed = (
        P("grp", ("seq", "head"), None),
        P("grp", ("seq", "head"), None),
        P(("seq", "head"), None, None),
        P(("seq", "head"), None, None),
        P("grp", "seq", None),
        P("grp"),
        P("grp", None, None),
    )
    return jax.shard_map(
        local,
        mesh=mesh,
        in_specs=placed,
        out_specs=(P("grp", ("seq", "head"), None), P("grp", None, "seq")),
        check_vma=False,
    )
```
